32 devices in a mesh: ctx: 8 (over y, x, core), tp: 4 (over z).
Axes of the slice: x: 2, y: 2, z: 4, core: 2. Of those that a mesh axis runs over, the one named last changes fastest.
Arguments:
- layer_in: bfloat16 [8192, 1024], P(('ctx', 'tp')), may hold values from -6 to 6
- gain_one: float32 [1024], replicated, may hold values from 0.5 to 1.5
- w_query: bfloat16 [1024, 1024], P(None, 'tp'), may hold values from -0.1875 to 0.1875
- w_key: bfloat16 [1024, 1024], P(None, 'tp'), may hold values from -0.1875 to 0.1875
- w_value: bfloat16 [1024, 1024], P(None, 'tp'), may hold values from -0.1875 to 0.1875
- w_out: bfloat16 [1024, 1024], P('tp'), may hold values from -3 to 3
- bias_table: float32 [32, 16], P(None, 'tp'), may hold values from -4 to 4
- gain_two: float32 [1024], replicated, may hold values from 0.5 to 1.5
- w_router: bfloat16 [1024, 4], replicated, may hold values from -0.125 to 0.125
- w_gate: bfloat16 [4, 1024, 2816], P(None, None, 'tp'), may hold values from -0.1875 to 0.1875
- w_up: bfloat16 [4, 1024, 2816], P(None, None, 'tp'), may hold values from -0.1875 to 0.1875
- w_down: bfloat16 [4, 2816, 1024], P(None, 'tp'), may hold values from -0.3125 to 0.3125
- lengths: int32 [16], replicated, may hold values from 1 to 6144, 8192 in all
- block_perm: int32 [64], replicated, may hold values from 0 to 63, as said below
- buckets: int32 [128], replicated, may hold values from 0 to 31, as said below
- routes: int32 [8192, 2], P('ctx'), may hold values from 0 to 3, as said below
- cotangent: bfloat16 [8192, 1024], P(('ctx', 'tp')), may hold values from -6 to 6
Outputs:
- layer_out: float32 [8192, 1024], P(('ctx', 'tp'))
- grad_x: float32 [8192, 1024], P(('ctx', 'tp'))
- grad_gain_one: float32 [1024], P('tp')
- grad_w_query: float32 [1024, 1024], P(None, 'tp')
- grad_w_key: float32 [1024, 1024], P(None, 'tp')
- grad_w_value: float32 [1024, 1024], P(None, 'tp')
- grad_w_out: float32 [1024, 1024], P('tp')
- grad_table: float32 [32, 16], P(None, 'tp')
- grad_gain_two: float32 [1024], P('tp')
- grad_w_router: float32 [1024, 4], P('tp')
- grad_w_gate: float32 [4, 1024, 2816], P(None, None, 'tp')
- grad_w_up: float32 [4, 1024, 2816], P(None, None, 'tp')
- grad_w_down: float32 [4, 2816, 1024], P(None, 'tp')
The draws below stay inside these ranges and needn't reach their ends.
Inputs may be any that keep to these rules, and one draw needn't show every extreme that they name: `lengths`: 16 sequences packed end to end in this order; exactly one has the greatest length 6144 or several have it. A permutation: stored block j of every token array is packed block block_perm[j]; for even j, block_perm[j + 1] = 63 - block_perm[j]. `buckets`: bucket of each distance of 0 to 127 tokens; larger distances take the last entry. Starts at 0, never falls, rises by 0 or 1 from one distance to the next, ends at 31. `routes`: each row names 2 different experts.
All inputs are finite; a program needn't handle non-finite values.
Results may differ from the reference program's by a relative error of at most 0.03.
Values may be sent and summed in bfloat16 or wider, within the bound.
No kernel may reach another device: no remote copies, remote signals or barrier semaphores. Data moves between devices by JAX's collectives and lax.ppermute only.
A program may use at most 192 MiB of HBM per device.

```python
import math
import jax
import jax.numpy as jnp
import numpy as np
from jax import lax

D = 1024
H = 16
DH = 64
FF = 2816
EXPERTS = 4
TOPK = 2
BLOCK = 128
NBUCKET = 32
TOK_CTX = 1024
TOKENS = 8192
NSEQ = 16
MAXLEN = 6144
NBLK = 64
HD = 1024
CAP = 640
TILE = 512
N_CTX = 8


def draw_block_perm(key, part):
    key = jax.random.fold_in(key, 11)
    rounds = TOKENS // BLOCK // 2 // N_CTX
    round_keys = jax.random.split(key, rounds)
    shuffles = jax.vmap(lambda one_key: jax.random.permutation(one_key, N_CTX))(round_keys)
    first_half = jnp.arange(rounds, dtype=jnp.int32)[None, :] * N_CTX + shuffles.T.astype(jnp.int32)
    mirrored = TOKENS // BLOCK - 1 - first_half
    return jnp.stack([first_half, mirrored], axis=2).reshape(-1).astype(jnp.int32)


def draw_buckets(key, part):
    key = jax.random.fold_in(key, 23)
    ordering = jax.random.permutation(key, BLOCK - 1)
    rising = (ordering < NBUCKET - 1).astype(jnp.int32)
    return jnp.concatenate([jnp.zeros((1,), jnp.int32), jnp.cumsum(rising)]).astype(jnp.int32)


def draw_routes(key, part):
    key = jax.random.fold_in(key, 37)
    keys = jax.random.split(key, 4)
    groups = TOKENS // TOK_CTX
    favoured = jnp.repeat(jax.random.randint(keys[0], (groups,), 0, EXPERTS), TOK_CTX, total_repeat_length=TOKENS)
    leaning = jax.random.randint(keys[1], (TOKENS,), 0, 100) < 36
    first = jnp.where(leaning, favoured, jax.random.randint(keys[2], (TOKENS,), 0, EXPERTS))
    second = (first + jax.random.randint(keys[3], (TOKENS,), 1, EXPERTS)) % EXPERTS
    return jnp.stack([first, second], axis=1).astype(jnp.int32)


def block_levels(own_key, extent, cuts, least, top_value):
    def one(axis_at, parts):
        draws = jax.random.uniform(jax.random.fold_in(jax.random.fold_in(own_key, 6), axis_at), (parts,), jnp.float32, least / len(cuts), top_value / len(cuts))
        return jnp.repeat(jnp.exp(draws), extent[axis_at] // parts).reshape((-1,) + (1,) * (len(extent) - axis_at - 1))

    level = one(*cuts[0])
    for cut in cuts[1:]:
        level = level * one(*cut)
    return level


def length_profile(amount, total, bound, skew):
    weights = [(1 << 20) // math.isqrt(grade ** skew) + 1 for grade in range(2, amount + 1)]
    rest, holding = total - bound - (amount - 1), [1] * (amount - 1)
    while rest > 0:
        movable = [i for i in range(amount - 1) if holding[i] < bound]
        pool, remaining = sum([weights[i] for i in movable]), rest
        for i in movable:
            more = min(bound - holding[i], max(1, remaining * weights[i] // pool), rest)
            holding[i] = holding[i] + more
            rest = rest - more
    return np.array([bound] + holding)


def ragged_sizes(rng, amount, total, limit, lean):
    if amount == 2:
        one = jax.random.randint(rng, (), max(1, total - limit), min(limit, total - 1) + 1)
        return jnp.stack([one, total - one])
    tallies = jnp.asarray(length_profile(amount, total, limit, lean), jnp.int32)
    pairs = (amount - 1) // 2
    giver, sink = tallies[1:1 + 2 * pairs:2], tallies[2:2 + 2 * pairs:2]
    margin = jnp.minimum(giver - 1, limit - sink)
    passed = jax.random.randint(jax.random.fold_in(rng, 1), (pairs,), 0, 1 << 20) % (margin + 1)
    tallies = tallies.at[1:1 + 2 * pairs:2].set(giver - passed).at[2:2 + 2 * pairs:2].set(sink + passed)
    return tallies[jax.random.permutation(jax.random.fold_in(rng, 2), amount)]


def scatter_about(stream_key, extent, deviation, most, shards=(), kind=jnp.bfloat16):
    result = jax.random.normal(stream_key, extent, jnp.float32) * deviation
    if len(shards) > 0:
        result = block_levels(stream_key, extent, shards, -0.22, 0.18) * result
    return jnp.clip(result, min=-most, max=most).astype(kind)


def setup_inputs(seed: int = 0) -> dict:
    splits = jax.random.split(jax.random.key(seed), 18)
    return {
        "layer_in": scatter_about(splits[0], (TOKENS, D), 1.0, 6.0, ((0, 32),)),
        "gain_one": jnp.clip(1.0 + 0.1 * jax.random.normal(splits[1], (D,), jnp.float32), 0.5, 1.5),
        "w_query": scatter_about(splits[2], (D, HD), D ** -0.5, 0.1875, ((1, 4),)),
        "w_key": scatter_about(splits[3], (D, HD), D ** -0.5, 0.1875, ((1, 4),)),
        "w_value": scatter_about(splits[4], (D, HD), D ** -0.5, 0.1875, ((1, 4),)),
        "w_out": scatter_about(splits[5], (HD, D), 4 ** -0.5, 3.0, ((0, 4),)),
        "bias_table": scatter_about(splits[6], (NBUCKET, H), 1.0, 4.0, ((1, 4),), jnp.float32),
        "gain_two": jnp.clip(1.0 + 0.1 * jax.random.normal(splits[7], (D,), jnp.float32), 0.5, 1.5),
        "w_router": scatter_about(splits[8], (D, EXPERTS), (2 * D) ** -0.5, 0.125),
        "w_gate": scatter_about(splits[9], (EXPERTS, D, FF), D ** -0.5, 0.1875, ((2, 4),)),
        "w_up": scatter_about(splits[10], (EXPERTS, D, FF), D ** -0.5, 0.1875, ((2, 4),)),
        "w_down": scatter_about(splits[11], (EXPERTS, FF, D), (FF // 8) ** -0.5, 0.3125, ((1, 4),)),
        "lengths": ragged_sizes(splits[12], NSEQ, TOKENS, MAXLEN, 1).astype(jnp.int32),
        "block_perm": draw_block_perm(jax.random.fold_in(splits[17], 71), 0),
        "buckets": draw_buckets(jax.random.fold_in(splits[17], 71), 0),
        "routes": draw_routes(jax.random.fold_in(splits[17], 71), 0),
        "cotangent": scatter_about(splits[16], (TOKENS, D), 1.0, 6.0, ((0, 32),)),
    }


EPS = 1e-06
NEG = -1e+30
HIGH = lax.Precision.HIGHEST

@jax.custom_vjp
def low(v):
    return lax.optimization_barrier(v.astype(jnp.bfloat16)).astype(jnp.float32)

@jax.custom_vjp
def low_back(v):
    return v

def low_keep(v):
    return (low(v), None)

def low_pass(kept, grad):
    return (grad,)

def back_keep(v):
    return (v, None)

def back_low(kept, grad):
    return (low(grad),)
low.defvjp(low_keep, low_pass)
low_back.defvjp(back_keep, back_low)

def matmul(left, right):
    return jnp.dot(left, right, precision=HIGH, preferred_element_type=jnp.float32)

def rms_scale(values):
    return lax.rsqrt(lax.optimization_barrier(jnp.mean(values * values, axis=-1, keepdims=True)) + EPS)

def slot_tables(group_routes):
    count = group_routes.shape[0]
    flat = group_routes.T.reshape(-1)
    hot = (flat[:, None] == jnp.arange(EXPERTS, dtype=jnp.int32)[None, :]).astype(jnp.int32)
    rank_of = lax.optimization_barrier(jnp.sum((jnp.cumsum(hot, axis=0) - hot) * hot, axis=1))
    kept = rank_of < CAP
    dest = jnp.where(kept, flat * CAP + rank_of, EXPERTS * CAP).astype(jnp.int32)
    tokens = jnp.tile(jnp.arange(count, dtype=jnp.int32), TOPK)
    token_of_slot = jnp.zeros((EXPERTS * CAP + 1,), jnp.int32).at[dest].set(tokens)[:EXPERTS * CAP]
    live = jnp.zeros((EXPERTS * CAP + 1,), jnp.float32).at[dest].set(1.0)[:EXPERTS * CAP]
    return (dest, kept.reshape(TOPK, count).astype(jnp.float32), token_of_slot, live)

def natural_order(values, inverse):
    return values.reshape(NBLK, BLOCK, H, DH)[inverse].reshape(TOKENS, H, DH)

def attention(queries, keys, values, bias_table, buckets, owners, inverse, block_perm):
    window = MAXLEN + TILE
    near_width = TILE + BLOCK
    dist_bias = bias_table[buckets]
    far_bias = dist_bias[BLOCK - 1]
    row_ids = jnp.arange(TILE, dtype=jnp.int32)[:, None]
    col_ids = jnp.arange(near_width, dtype=jnp.int32)[None, :]
    near_bias = jnp.transpose(dist_bias[jnp.clip(row_ids + BLOCK - col_ids, 0, BLOCK - 1)], (2, 0, 1))
    all_bias = jnp.concatenate([jnp.broadcast_to(far_bias[:, None, None], (H, TILE, window - near_width)), near_bias], axis=2)
    q_nat = natural_order(queries, inverse)
    padding = jnp.zeros((window, H, DH), queries.dtype)
    k_pad = jnp.concatenate([padding, natural_order(keys, inverse)], axis=0)
    v_pad = jnp.concatenate([padding, natural_order(values, inverse)], axis=0)
    owner_pad = jnp.concatenate([jnp.full((window,), -1, jnp.int32), owners])
    score_scale = DH ** (-0.5)

    def one_block(start):
        q_block = lax.dynamic_slice_in_dim(q_nat, start, TILE, 0)
        k_block = lax.dynamic_slice_in_dim(k_pad, start + TILE, window, 0)
        v_block = lax.dynamic_slice_in_dim(v_pad, start + TILE, window, 0)
        q_owner = lax.dynamic_slice_in_dim(owners, start, TILE, 0)
        k_owner = lax.dynamic_slice_in_dim(owner_pad, start + TILE, window, 0)
        distance = jnp.arange(TILE, dtype=jnp.int32)[:, None] - jnp.arange(window, dtype=jnp.int32)[None, :] + (window - TILE)
        allowed = (q_owner[:, None] == k_owner[None, :]) & (distance >= 0)
        scores = jnp.einsum('qhd,khd->hqk', q_block, k_block, precision=HIGH) * score_scale + all_bias
        scores = low_back(scores)
        scores = jnp.where(allowed[None], scores, NEG)
        highest = lax.optimization_barrier(jnp.max(scores, axis=2, keepdims=True))
        expo = jnp.exp(scores - highest)
        probs = low(expo / lax.optimization_barrier(jnp.sum(expo, axis=2, keepdims=True)))
        return jnp.einsum('hqk,khd->qhd', probs, v_block, precision=HIGH)
    starts = jnp.arange(TOKENS // TILE, dtype=jnp.int32) * TILE
    attended = lax.map(jax.checkpoint(one_block), starts).reshape(TOKENS, H, DH)
    return attended.reshape(NBLK, BLOCK, H * DH)[block_perm].reshape(TOKENS, H * DH)

def reference(layer_in, gain_one, w_query, w_key, w_value, w_out, bias_table, gain_two, w_router, w_gate, w_up, w_down, lengths, block_perm, buckets, routes, cotangent):
    group_tables = jax.vmap(slot_tables)(routes.reshape(N_CTX, TOK_CTX, TOPK))
    ends = jnp.cumsum(lengths).astype(jnp.int32)
    places = jnp.arange(TOKENS, dtype=jnp.int32)
    owners = lax.optimization_barrier(jnp.sum((ends[None, :] <= places[:, None]).astype(jnp.int32), axis=1))
    inverse = jnp.zeros((NBLK,), jnp.int32).at[block_perm].set(jnp.arange(NBLK, dtype=jnp.int32))

    def forward(x_in, gain_a, query_w, key_w, value_w, out_w, table, gain_b, router_w, gate_w, up_w, down_w):
        h_one = low(x_in * rms_scale(x_in) * gain_a)

        def project(weight):
            return low(low_back(matmul(h_one, weight))).reshape(TOKENS, H, DH)
        attended = attention(project(query_w), project(key_w), project(value_w), table, buckets, owners, inverse, block_perm)
        attended = low(low_back(attended))
        mixed_in = x_in + low_back(matmul(attended, out_w))
        h_two = low(mixed_in * rms_scale(mixed_in) * gain_b)
        logits = matmul(h_two, router_w)
        highest = lax.optimization_barrier(jnp.max(logits, axis=1, keepdims=True))
        expo = jnp.exp(logits - highest)
        gates = expo / lax.optimization_barrier(jnp.sum(expo, axis=1, keepdims=True))

        def expert_group(operands):
            rows, probs, group_routes, dest, kept, token_of_slot, live = operands
            inputs = (rows[token_of_slot] * live[:, None]).reshape(EXPERTS, CAP, D)
            gate_pre = low_back(jnp.einsum('ecd,edf->ecf', inputs, gate_w, precision=HIGH))
            up_pre = low_back(jnp.einsum('ecd,edf->ecf', inputs, up_w, precision=HIGH))
            hidden = low(jax.nn.gelu(gate_pre, approximate=True) * up_pre)
            outputs = low_back(jnp.einsum('ecf,efd->ecd', hidden, down_w, precision=HIGH)).reshape(EXPERTS * CAP, D)
            chosen = (group_routes.T[:, :, None] == jnp.arange(EXPERTS, dtype=jnp.int32)[None, None, :]).astype(probs.dtype)
            picked = lax.optimization_barrier(jnp.sum(probs[None] * chosen, axis=2)) * kept
            gathered = outputs[jnp.minimum(dest, EXPERTS * CAP - 1)].reshape(TOPK, TOK_CTX, D)
            return lax.optimization_barrier(jnp.sum(picked[:, :, None] * gathered, axis=0))
        mixed = lax.map(jax.checkpoint(expert_group), (h_two.reshape(N_CTX, TOK_CTX, D), gates.reshape(N_CTX, TOK_CTX, EXPERTS), routes.reshape(N_CTX, TOK_CTX, TOPK)) + tuple(group_tables))
        return mixed_in + mixed.reshape(TOKENS, D)
    floats = (layer_in.astype(jnp.float32), gain_one.astype(jnp.float32), w_query.astype(jnp.float32), w_key.astype(jnp.float32), w_value.astype(jnp.float32), w_out.astype(jnp.float32), bias_table.astype(jnp.float32), gain_two.astype(jnp.float32), w_router.astype(jnp.float32), w_gate.astype(jnp.float32), w_up.astype(jnp.float32), w_down.astype(jnp.float32))
    layer_out, pull = jax.vjp(forward, *floats)
    grads = pull(cotangent.astype(jnp.float32))
    return (layer_out, grads[0], grads[1], grads[2], grads[3], grads[4], grads[5], grads[6], grads[7], grads[8], grads[9], grads[10], grads[11])
```

```python
import functools

import jax
import jax.numpy as jnp
from jax import lax
from jax.experimental import pallas as pl
from jax.experimental.pallas import tpu as pltpu
from jax.sharding import PartitionSpec as P

DH = 64
BLOCK = 128


EPS = 1e-06
NEG = -1e30
HIGH = lax.Precision.HIGHEST


LOG2E = 1.4426950408889634
KT = 512
VMEM_LIMIT = 56 * 1024 * 1024


def dot(left, right):
    return jnp.dot(left, right, preferred_element_type=jnp.float32)


def place_pairs(nat_ref, part_refs, k_row, count, keys_flat, keys_tall):
    keys_flat[:, :BLOCK] = jnp.zeros((2 * DH, BLOCK), keys_flat.dtype)
    keys_tall[:BLOCK, :] = jnp.zeros((BLOCK, 2 * DH), keys_tall.dtype)
    for part, ref in enumerate(part_refs):
        row = k_row if part == 0 else 0

        def one(index, _, part=part, ref=ref, row=row):
            at = pl.multiple_of((nat_ref[part * count + index] + 1) * BLOCK, BLOCK)
            pair = ref[index, row : row + 2 * DH, :]
            keys_flat[:, pl.ds(at, BLOCK)] = pair
            keys_tall[pl.ds(at, BLOCK), :] = pair.T
            return 0

        lax.fori_loop(0, count, one, 0)


def fill_near_bias(thr_ref, tab_ref, near_bias, bucket_count):
    key_ids = lax.broadcasted_iota(jnp.int32, (2 * BLOCK, BLOCK), 0)
    query_ids = lax.broadcasted_iota(jnp.int32, (2 * BLOCK, BLOCK), 1)
    distance = query_ids + BLOCK - key_ids
    value = jnp.full((2 * BLOCK, BLOCK), tab_ref[0], jnp.float32)
    for bucket in range(1, bucket_count):
        value = jnp.where(distance >= thr_ref[bucket], tab_ref[bucket], value)
    near_bias[...] = jnp.where(distance >= 0, value, NEG)


def pair_ids(nat_ref, tile, order_ref):
    slot_a = order_ref[2 * tile]
    slot_b = order_ref[2 * tile + 1]
    return slot_a, slot_b, nat_ref[slot_a], nat_ref[slot_b]


def lane_pair(first, second):
    return jnp.concatenate([first, second], axis=1)


def forward_kernel(
    bucket_count,
    parts,
    nat_ref,
    order_ref,
    low_ref,
    thr_ref,
    tab_ref,
    seq_ref,
    *rest,
):
    part_refs = rest[:parts]
    out_ref, full_ref, lse_ref = rest[parts : parts + 3]
    keys_flat, keys_tall, near_bias = rest[parts + 3 :]
    own_ref = part_refs[0]
    count = own_ref.shape[0]
    total = keys_tall.shape[0] - BLOCK
    scale = DH ** (-0.5) * LOG2E
    bf16 = jnp.bfloat16
    place_pairs(nat_ref, part_refs, DH, count, keys_flat, keys_tall)
    fill_near_bias(thr_ref, tab_ref, near_bias, bucket_count)
    near_ids = lax.broadcasted_iota(jnp.int32, (2 * BLOCK, BLOCK), 0)
    far_ids = lax.broadcasted_iota(jnp.int32, (KT, 2 * BLOCK), 0)

    def one_tile(tile, _):
        slot_a, slot_b, blk_a, blk_b = pair_ids(nat_ref, tile, order_ref)
        q_pair = lane_pair(own_ref[slot_a, :DH, :], own_ref[slot_b, :DH, :])
        q_wide = jnp.concatenate([q_pair, jnp.zeros_like(q_pair)], axis=0)
        starts = []
        stats = []
        for half, blk in enumerate((blk_a, blk_b)):
            at = pl.multiple_of(blk * BLOCK, BLOCK)
            start = seq_ref[pl.ds(blk, 1), :]
            starts.append(start)
            s = dot(
                keys_tall[pl.ds(at, 2 * BLOCK), :],
                q_wide[:, half * BLOCK : (half + 1) * BLOCK],
            )
            s = s * scale + near_bias[...]
            s = jnp.where(near_ids >= start - (blk - 1) * BLOCK, s, NEG)
            top = jnp.max(s, axis=0, keepdims=True)
            p = jnp.exp2(s - top)
            acc = dot(keys_flat[DH:, pl.ds(at, 2 * BLOCK)], p.astype(bf16))
            stats.append((top, jnp.sum(p, axis=0, keepdims=True), acc))
        top = lane_pair(stats[0][0], stats[1][0])
        norm = lane_pair(stats[0][1], stats[1][1])
        acc = lane_pair(stats[0][2], stats[1][2])
        start = lane_pair(*starts)
        lane = lax.broadcasted_iota(jnp.int32, (1, 2 * BLOCK), 1)
        stop = jnp.where(lane < BLOCK, (blk_a - 1) * BLOCK, (blk_b - 1) * BLOCK)
        first = low_ref[blk_a] * BLOCK
        steps = (jnp.maximum((blk_b - 1) * BLOCK - first, 0) + KT - 1) // KT

        def far(step, carry):
            top, norm, acc = carry
            begin = first + step * KT
            at = jnp.minimum(begin, total - KT)
            here = pl.multiple_of(at + BLOCK, BLOCK)
            s = dot(keys_tall[pl.ds(here, KT), :], q_wide)
            valid = (far_ids >= jnp.maximum(start, begin) - at) & (far_ids < stop - at)
            s = jnp.where(valid, s * scale, NEG)
            new_top = jnp.maximum(top, jnp.max(s, axis=0, keepdims=True))
            p = jnp.exp2(s - new_top)
            factor = jnp.exp2(top - new_top)
            norm = norm * factor + jnp.sum(p, axis=0, keepdims=True)
            acc = acc * factor + dot(keys_flat[DH:, pl.ds(here, KT)], p.astype(bf16))
            return new_top, norm, acc

        top, norm, acc = lax.fori_loop(0, steps, far, (top, norm, acc))
        result = acc / norm
        lse = top + jnp.log(norm) * LOG2E
        for half, slot in enumerate((slot_a, slot_b)):
            part = result[:, half * BLOCK : (half + 1) * BLOCK]
            full_ref[pl.ds(slot, 1)] = part[None]
            out_ref[pl.ds(slot, 1)] = part.astype(bf16)[None]
            lse_ref[pl.ds(slot, 1), :] = lse[:, half * BLOCK : (half + 1) * BLOCK]
        return 0

    lax.fori_loop(0, count // 2, one_tile, 0)


def backward_kernel(
    bucket_count,
    parts,
    nat_ref,
    order_ref,
    low_ref,
    thr_ref,
    tab_ref,
    seq_ref,
    *rest,
):
    part_refs = rest[:parts]
    dout_ref, full_ref, lse_ref = rest[parts : parts + 3]
    dq_ref = rest[parts + 3]
    dkv_refs = rest[parts + 4 : 2 * parts + 4]
    table_ref = rest[2 * parts + 4]
    keys_flat, keys_tall, near_bias, grads, near_grads = rest[2 * parts + 5 :]
    own_ref = part_refs[0]
    count = own_ref.shape[0]
    total = keys_tall.shape[0] - BLOCK
    scale = DH ** (-0.5) * LOG2E
    bf16 = jnp.bfloat16
    f32 = jnp.float32
    place_pairs(nat_ref, part_refs, DH, count, keys_flat, keys_tall)
    fill_near_bias(thr_ref, tab_ref, near_bias, bucket_count)
    grads[...] = jnp.zeros_like(grads)
    near_grads[...] = jnp.zeros_like(near_grads)
    near_ids = lax.broadcasted_iota(jnp.int32, (2 * BLOCK, BLOCK), 0)
    far_ids = lax.broadcasted_iota(jnp.int32, (KT, 2 * BLOCK), 0)
    low_lane = lax.broadcasted_iota(jnp.int32, (BLOCK, 2 * DH), 1) < DH

    def one_tile(tile, _):
        slot_a, slot_b, blk_a, blk_b = pair_ids(nat_ref, tile, order_ref)
        starts, lses, sums, rights, out_sides, q_sides, dq_near = [], [], [], [], [], [], []
        for slot, blk in ((slot_a, blk_a), (slot_b, blk_b)):
            at = pl.multiple_of(blk * BLOCK, BLOCK)
            start = seq_ref[pl.ds(blk, 1), :]
            q_t = own_ref[slot, :DH, :]
            do_t = dout_ref[slot]
            lse = lse_ref[pl.ds(slot, 1), :]
            dsum = jnp.sum(do_t.astype(f32) * full_ref[slot], axis=0, keepdims=True)
            zero = jnp.zeros_like(q_t)
            right = lane_pair(
                jnp.concatenate([q_t, zero], axis=0), jnp.concatenate([zero, do_t], axis=0)
            )
            both = jnp.concatenate([q_t, do_t], axis=0).T
            none = jnp.zeros_like(both)
            q_side = jnp.where(low_lane, both, none)
            out_side = jnp.where(low_lane, none, both)
            s_dp = dot(keys_tall[pl.ds(at, 2 * BLOCK), :], right)
            s = s_dp[:, :BLOCK] * scale + near_bias[...]
            s = jnp.where(near_ids >= start - (blk - 1) * BLOCK, s, NEG)
            p = jnp.exp2(s - lse)
            ds = (p * (s_dp[:, BLOCK:] - dsum)).astype(bf16)
            grads[pl.ds(at, 2 * BLOCK), :] += dot(
                lane_pair(p.astype(bf16), ds), jnp.concatenate([out_side, q_side], axis=0)
            )
            near_grads[...] += ds.astype(f32)
            dq_near.append(dot(keys_flat[:DH, pl.ds(at, 2 * BLOCK)], ds))
            starts.append(start)
            lses.append(lse)
            sums.append(dsum)
            rights.append(right)
            out_sides.append(out_side)
            q_sides.append(q_side)
        start = lane_pair(*starts)
        lse = lane_pair(*lses)
        dsum = lane_pair(*sums)
        right = jnp.concatenate(
            [
                rights[0][:, :BLOCK],
                rights[1][:, :BLOCK],
                rights[0][:, BLOCK:],
                rights[1][:, BLOCK:],
            ],
            axis=1,
        )
        sides = jnp.concatenate(out_sides + q_sides, axis=0)
        lane = lax.broadcasted_iota(jnp.int32, (1, 2 * BLOCK), 1)
        stop = jnp.where(lane < BLOCK, (blk_a - 1) * BLOCK, (blk_b - 1) * BLOCK)
        first = low_ref[blk_a] * BLOCK
        steps = (jnp.maximum((blk_b - 1) * BLOCK - first, 0) + KT - 1) // KT

        def far(step, dq):
            begin = first + step * KT
            at = jnp.minimum(begin, total - KT)
            here = pl.multiple_of(at + BLOCK, BLOCK)
            s_dp = dot(keys_tall[pl.ds(here, KT), :], right)
            valid = (far_ids >= jnp.maximum(start, begin) - at) & (far_ids < stop - at)
            s = jnp.where(valid, s_dp[:, : 2 * BLOCK] * scale, NEG)
            p = jnp.exp2(s - lse)
            ds = (p * (s_dp[:, 2 * BLOCK :] - dsum)).astype(bf16)
            grads[pl.ds(here, KT), :] += dot(lane_pair(p.astype(bf16), ds), sides)
            return dq + dot(keys_flat[:DH, pl.ds(here, KT)], ds)

        dq = lax.fori_loop(0, steps, far, lane_pair(*dq_near)) * DH ** (-0.5)
        for half, slot in enumerate((slot_a, slot_b)):
            part = dq[:, half * BLOCK : (half + 1) * BLOCK]
            dq_ref[pl.ds(slot, 1)] = part.astype(bf16)[None]
        return 0

    lax.fori_loop(0, count // 2, one_tile, 0)
    key_lane = jnp.where(low_lane, DH ** (-0.5), 1.0)
    for part in range(parts):

        def give(index, _, part=part):
            at = pl.multiple_of((nat_ref[part * count + index] + 1) * BLOCK, BLOCK)
            block = grads[pl.ds(at, BLOCK), :] * key_lane
            dkv_refs[part][pl.ds(index, 1)] = block.T.astype(bf16)[None]
            return 0

        lax.fori_loop(0, count, give, 0)
    key_ids = lax.broadcasted_iota(jnp.int32, (2 * BLOCK, BLOCK), 0)
    query_ids = lax.broadcasted_iota(jnp.int32, (2 * BLOCK, BLOCK), 1)
    distance = query_ids + BLOCK - key_ids
    near = near_grads[...]
    out_lane = lax.broadcasted_iota(jnp.int32, (1, BLOCK), 1)
    above = jnp.sum(near, axis=(0, 1), keepdims=True)
    result = jnp.zeros((1, BLOCK), f32)
    seen = jnp.zeros((1, 1), f32)
    for bucket in range(1, bucket_count):
        kept = jnp.sum(
            jnp.where(distance >= thr_ref[bucket], near, 0.0), axis=(0, 1), keepdims=True
        )
        result = jnp.where(out_lane == bucket - 1, above - kept, result)
        seen = seen + (above - kept)
        above = kept
    table_ref[...] = jnp.where(out_lane == bucket_count - 1, -seen, result)


def attention_call(kernel, parts, bucket_count, scalars, seq_start, arrays, out_shape, total, extra):
    smem = pl.BlockSpec(memory_space=pltpu.SMEM)
    vmem = pl.BlockSpec(memory_space=pltpu.VMEM)
    operands = list(scalars) + [seq_start] + list(arrays)
    scratch = [
        pltpu.VMEM((2 * DH, total + BLOCK), jnp.bfloat16),
        pltpu.VMEM((total + BLOCK, 2 * DH), jnp.bfloat16),
        pltpu.VMEM((2 * BLOCK, BLOCK), jnp.float32),
    ] + extra
    return pl.pallas_call(
        functools.partial(kernel, bucket_count, parts),
        out_shape=out_shape,
        in_specs=[smem] * len(scalars) + [vmem] * (1 + len(arrays)),
        out_specs=[vmem] * len(out_shape),
        scratch_shapes=scratch,
        compiler_params=pltpu.CompilerParams(vmem_limit_bytes=VMEM_LIMIT),
    )(*operands)


def turn_halves(x, axis, amounts, sign):
    halves = x.shape[axis + 1]
    shape = [1] * x.ndim
    shape[axis] = x.shape[axis]
    amounts = amounts.reshape(shape)
    result = x
    for step in range(1, halves):
        result = jnp.where(amounts == step, jnp.roll(x, -sign * step, axis=axis + 1), result)
    return result


def slot_tables(group_routes, experts, capacity):
    count = group_routes.shape[0]
    top_count = group_routes.shape[1]
    flat = group_routes.T.reshape(-1)
    hot = (flat[:, None] == jnp.arange(experts, dtype=jnp.int32)[None, :]).astype(jnp.int32)
    rank_of = jnp.sum((jnp.cumsum(hot, axis=0) - hot) * hot, axis=1)
    kept = rank_of < capacity
    dest = jnp.where(kept, flat * capacity + rank_of, experts * capacity)
    tokens = jnp.tile(jnp.arange(count, dtype=jnp.int32), top_count)
    token_of_slot = (
        jnp.zeros((experts * capacity + 1,), jnp.int32).at[dest].set(tokens)[: experts * capacity]
    )
    live = jnp.zeros((experts * capacity + 1,), jnp.float32).at[dest].set(1.0)[: experts * capacity]
    return (dest, kept.reshape(top_count, count).astype(jnp.float32), token_of_slot, live)


def on_device(
    layer_in,
    gain_one,
    w_query,
    w_key,
    w_value,
    w_out,
    bias_table,
    gain_two,
    w_router,
    w_gate,
    w_up,
    w_down,
    lengths,
    block_perm,
    buckets,
    routes,
    cotangent,
):
    tp_count = lax.axis_size("tp")
    ctx_count = lax.axis_size("ctx")
    tp_index = lax.axis_index("tp")
    ctx_index = lax.axis_index("ctx")
    rows_dev = layer_in.shape[0]
    width = layer_in.shape[1]
    group_rows = rows_dev * tp_count
    width_loc = w_query.shape[1]
    head_count = width_loc // DH
    blocks_group = group_rows // BLOCK
    experts = w_gate.shape[0]
    top_count = routes.shape[1]
    capacity = 5 * top_count * group_rows // (4 * experts)
    slot_count = experts * capacity
    bucket_count = bias_table.shape[0]
    f32 = jnp.float32
    bf16 = jnp.bfloat16
    x_float = layer_in.astype(f32)
    inv_one = lax.rsqrt(jnp.mean(x_float * x_float, axis=1, keepdims=True) + EPS)
    normed_one = x_float * inv_one
    h_one = (normed_one * gain_one).astype(bf16)
    h_one_all = lax.all_gather(h_one, "tp", axis=0, tiled=True)
    w_qkv = jnp.concatenate([w_query, w_key, w_value], axis=1)
    qkv = lax.dot_general(
        w_qkv, h_one_all, (((0,), (1,)), ((), ())), preferred_element_type=f32
    ).astype(bf16)
    team = ctx_count // head_count
    member = ctx_index % team
    my_head = ctx_index // team
    pair_count = blocks_group // team
    slot_blocks = ctx_count * pair_count
    total = ctx_count * group_rows
    pair_ids_m = jnp.arange(pair_count, dtype=jnp.int32)
    turn = (ctx_index + pair_ids_m) % team
    ends = jnp.cumsum(lengths)
    begins = ends - lengths
    places = jnp.arange(total, dtype=jnp.int32)
    seq_start = jnp.max(
        jnp.where(begins[None, :] <= places[:, None], begins[None, :], 0), axis=1
    ).reshape(total // BLOCK, BLOCK)
    low_block = seq_start[:, 0] // BLOCK
    thresholds = jnp.sum(
        (buckets[None, :] < jnp.arange(bucket_count, dtype=jnp.int32)[:, None]).astype(jnp.int32),
        axis=1,
    )
    head_hot = (jnp.arange(head_count, dtype=jnp.int32) == my_head).astype(f32)
    my_table = jnp.sum(bias_table * head_hot[None, :], axis=1)
    near_table = (my_table - my_table[bucket_count - 1]) * LOG2E
    sources = jnp.arange(ctx_count, dtype=jnp.int32)
    members = (member + jnp.arange(team, dtype=jnp.int32)) % team
    half_of = (members[:, None, None] + sources[None, :, None] + pair_ids_m[None, None, :]) % team
    perm_pairs = block_perm.reshape(1, ctx_count, pair_count, team)
    natural = jnp.sum(
        jnp.where(
            half_of[..., None] == jnp.arange(team, dtype=jnp.int32)[None, None, None, :],
            perm_pairs,
            0,
        ),
        axis=3,
    ).reshape(-1)
    own_natural = natural[:slot_blocks]
    rank = jnp.sum((own_natural[None, :] < own_natural[:, None]).astype(jnp.int32), axis=1)
    slots = jnp.arange(slot_blocks, dtype=jnp.int32)
    order = jnp.sum(jnp.where(rank[None, :] == slots[:, None], slots[None, :], 0), axis=1)
    scalars = (natural, order, low_block, thresholds, near_table)

    def to_heads(x, kinds):
        split = x.reshape(kinds, head_count, DH, pair_count, team, BLOCK)
        split = turn_halves(split, 3, turn, 1)
        send = split.transpose(1, 4, 3, 0, 2, 5).reshape(
            ctx_count, pair_count, kinds * DH, BLOCK
        )
        got = lax.all_to_all(send, "ctx", 0, 0, tiled=True)
        return got.reshape(slot_blocks, kinds * DH, BLOCK)

    def from_heads(x, kinds):
        send = x.reshape(ctx_count, pair_count, kinds * DH, BLOCK)
        got = lax.all_to_all(send, "ctx", 0, 0, tiled=True)
        split = got.reshape(head_count, team, pair_count, kinds, DH, BLOCK)
        split = split.transpose(3, 0, 4, 2, 1, 5)
        split = turn_halves(split, 3, turn, -1)
        return split.reshape(kinds * head_count * DH, group_rows)

    def team_shift(x, step):
        route = []
        for device in range(ctx_count):
            base = device // team * team
            route.append((device, base + (device % team + step) % team))
        return lax.ppermute(x, "ctx", route)

    own_qkv = to_heads(qkv, 3)
    own_pairs = own_qkv[:, DH:, :]
    parts = [own_qkv] + [team_shift(own_pairs, -step) for step in range(1, team)]
    head_block = (slot_blocks, DH, BLOCK)
    att_slots, att_full, log_total = attention_call(
        forward_kernel,
        team,
        bucket_count,
        scalars,
        seq_start,
        parts,
        [
            jax.ShapeDtypeStruct(head_block, bf16),
            jax.ShapeDtypeStruct(head_block, f32),
            jax.ShapeDtypeStruct((slot_blocks, BLOCK), f32),
        ],
        total,
        [],
    )
    attended_bf = from_heads(att_slots, 1)
    attn_rows = lax.psum_scatter(
        lax.dot_general(
            attended_bf, w_out, (((0,), (0,)), ((), ())), preferred_element_type=f32
        ).astype(jnp.bfloat16),
        "tp",
        scatter_dimension=0,
        tiled=True,
    ).astype(jnp.float32)
    mixed_in = x_float + attn_rows
    inv_two = lax.rsqrt(jnp.mean(mixed_in * mixed_in, axis=1, keepdims=True) + EPS)
    normed_two = mixed_in * inv_two
    h_two = (normed_two * gain_two).astype(bf16)
    h_two_all = lax.all_gather(h_two, "tp", axis=0, tiled=True)
    logits = jnp.dot(h_two_all, w_router, preferred_element_type=f32)
    expo = jnp.exp(logits - jnp.max(logits, axis=1, keepdims=True))
    gates = expo / jnp.sum(expo, axis=1, keepdims=True)
    dest, kept, token_of_slot, live = slot_tables(routes, experts, capacity)
    expert_ids = jnp.arange(experts, dtype=jnp.int32)
    chosen = (routes.T[:, :, None] == expert_ids[None, None, :]).astype(f32)
    picked = jnp.sum(gates[None] * chosen, axis=2) * kept
    weight_slot = jnp.zeros((slot_count + 1,), f32).at[dest].set(picked.reshape(-1))[:slot_count]
    expert_in = jnp.where(
        live[:, None] > 0, jnp.take(h_two_all, token_of_slot, axis=0), jnp.zeros((), bf16)
    ).reshape(experts, capacity, width)
    gate_pre = jnp.einsum("ecd,edf->ecf", expert_in, w_gate, preferred_element_type=f32)
    up_pre = jnp.einsum("ecd,edf->ecf", expert_in, w_up, preferred_element_type=f32)
    hidden = (jax.nn.gelu(gate_pre, approximate=True) * up_pre).astype(bf16)
    expert_out = jnp.einsum("ecf,efd->ecd", hidden, w_down, preferred_element_type=f32).reshape(
        slot_count, width
    )
    rows_back = jnp.take(expert_out, jnp.minimum(dest, slot_count - 1), axis=0).reshape(
        top_count, group_rows, width
    )
    mixed_part = jnp.sum(picked[:, :, None] * rows_back, axis=0)
    mixed_rows = lax.psum_scatter(
        mixed_part.astype(jnp.bfloat16), "tp", scatter_dimension=0, tiled=True
    ).astype(jnp.float32)
    layer_out = mixed_in + mixed_rows
    grad_float = cotangent.astype(f32)
    grad_all = lax.all_gather(cotangent, "tp", axis=0, tiled=True)
    gate_dots = jnp.sum(rows_back * grad_all.astype(f32)[None], axis=2)
    d_expert_out = (
        (jnp.take(grad_all, token_of_slot, axis=0).astype(f32) * weight_slot[:, None])
        .astype(bf16)
        .reshape(experts, capacity, width)
    )
    d_hidden = jnp.einsum("ecd,efd->ecf", d_expert_out, w_down, preferred_element_type=f32)
    grad_down = jnp.einsum("ecf,ecd->efd", hidden, d_expert_out, preferred_element_type=f32)
    _, glu_pull = jax.vjp(
        lambda gate_val, up_val: jax.nn.gelu(gate_val, approximate=True) * up_val, gate_pre, up_pre
    )
    d_gate_pre, d_up_pre = glu_pull(d_hidden)
    d_gate_bf = d_gate_pre.astype(bf16)
    d_up_bf = d_up_pre.astype(bf16)
    grad_gate = jnp.einsum("ecd,ecf->edf", expert_in, d_gate_bf, preferred_element_type=f32)
    grad_up = jnp.einsum("ecd,ecf->edf", expert_in, d_up_bf, preferred_element_type=f32)
    d_expert_in = (
        jnp.einsum("ecf,edf->ecd", d_gate_bf, w_gate, preferred_element_type=f32)
        + jnp.einsum("ecf,edf->ecd", d_up_bf, w_up, preferred_element_type=f32)
    ).reshape(slot_count, width)
    d_h_two_part = (
        jnp.zeros((group_rows, width), f32).at[token_of_slot].add(d_expert_in * live[:, None])
    )
    d_h_two, dots_own = (
        lax.psum_scatter(
            d_h_two_part.astype(jnp.bfloat16), "tp", scatter_dimension=0, tiled=True
        ).astype(jnp.float32),
        lax.psum_scatter(
            gate_dots.T.astype(jnp.bfloat16), "tp", scatter_dimension=0, tiled=True
        ).astype(jnp.float32),
    )
    own_start = tp_index * rows_dev
    gates_own = lax.dynamic_slice_in_dim(gates, own_start, rows_dev, 0)
    routes_own = lax.dynamic_slice_in_dim(routes, own_start, rows_dev, 0)
    kept_own = lax.dynamic_slice_in_dim(kept, own_start, rows_dev, 1)
    hot_own = (routes_own[:, :, None] == expert_ids[None, None, :]).astype(f32)
    d_gates = jnp.sum((dots_own * kept_own.T)[:, :, None] * hot_own, axis=1)
    d_logits = gates_own * (d_gates - jnp.sum(gates_own * d_gates, axis=1, keepdims=True))
    d_h_two = d_h_two + jnp.dot(
        d_logits, w_router.astype(f32).T, precision=HIGH, preferred_element_type=f32
    )
    grad_router_part = jnp.dot(h_two.T, d_logits, precision=HIGH, preferred_element_type=f32)
    d_norm_two = d_h_two * gain_two
    grad_gain_two_part = jnp.sum(d_h_two * normed_two, axis=0)
    d_mixed = grad_float + inv_two * (
        d_norm_two - normed_two * jnp.mean(d_norm_two * normed_two, axis=1, keepdims=True)
    )
    d_attn = d_mixed.astype(bf16)
    piece = lax.all_gather(d_attn, "tp", axis=0, tiled=True)
    d_attended = jnp.einsum("hd,rd->hr", w_out, piece, preferred_element_type=f32).astype(bf16)
    grad_out = jnp.einsum("hr,rd->hd", attended_bf, piece, preferred_element_type=f32)
    d_att_slots = to_heads(d_attended, 1)
    pair_block = jax.ShapeDtypeStruct((slot_blocks, 2 * DH, BLOCK), bf16)
    back = attention_call(
        backward_kernel,
        team,
        bucket_count,
        scalars,
        seq_start,
        parts + [d_att_slots, att_full, log_total],
        [jax.ShapeDtypeStruct(head_block, bf16)]
        + [pair_block] * team
        + [jax.ShapeDtypeStruct((1, BLOCK), f32)],
        total,
        [
            pltpu.VMEM((total + BLOCK, 2 * DH), f32),
            pltpu.VMEM((2 * BLOCK, BLOCK), f32),
        ],
    )
    pair_grads = back[1].astype(f32)
    for step in range(1, team):
        pair_grads = pair_grads + team_shift(back[1 + step], step).astype(f32)
    d_cat = from_heads(jnp.concatenate([back[0], pair_grads.astype(bf16)], axis=1), 3)
    grad_qkv = jnp.einsum("rd,hr->dh", h_one_all, d_cat, preferred_element_type=f32)
    grad_table_part = back[1 + team][0, :bucket_count, None] * head_hot[None, :]
    d_h_one_part = jnp.einsum("hr,dh->rd", d_cat, w_qkv, preferred_element_type=f32)
    d_h_one = lax.psum_scatter(
        d_h_one_part.astype(jnp.bfloat16), "tp", scatter_dimension=0, tiled=True
    ).astype(jnp.float32)
    d_norm_one = d_h_one * gain_one
    grad_gain_one_part = jnp.sum(d_h_one * normed_one, axis=0)
    grad_x = d_mixed + inv_one * (
        d_norm_one - normed_one * jnp.mean(d_norm_one * normed_one, axis=1, keepdims=True)
    )
    gain_one_share, gain_two_share, router_share = (
        lax.psum_scatter(grad_gain_one_part, "tp", scatter_dimension=0, tiled=True),
        lax.psum_scatter(grad_gain_two_part, "tp", scatter_dimension=0, tiled=True),
        lax.psum_scatter(grad_router_part, "tp", scatter_dimension=0, tiled=True),
    )
    rest_total = (
        lax.psum(grad_qkv[:, :width_loc].astype(jnp.bfloat16), "ctx").astype(jnp.float32),
        lax.psum(grad_qkv[:, width_loc : 2 * width_loc].astype(jnp.bfloat16), "ctx").astype(
            jnp.float32
        ),
        lax.psum(grad_qkv[:, 2 * width_loc :].astype(jnp.bfloat16), "ctx").astype(jnp.float32),
        lax.psum(grad_out.astype(jnp.bfloat16), "ctx").astype(jnp.float32),
        lax.psum(grad_table_part.astype(jnp.bfloat16), "ctx").astype(jnp.float32),
        lax.psum(gain_one_share.astype(jnp.bfloat16), "ctx").astype(jnp.float32),
        lax.psum(gain_two_share.astype(jnp.bfloat16), "ctx").astype(jnp.float32),
        lax.psum(router_share.astype(jnp.bfloat16), "ctx").astype(jnp.float32),
    )
    return (
        layer_out,
        grad_x,
        rest_total[5],
        rest_total[0],
        rest_total[1],
        rest_total[2],
        rest_total[3],
        rest_total[4],
        rest_total[6],
        rest_total[7],
        lax.psum(grad_gate.astype(jnp.bfloat16), "ctx").astype(jnp.float32),
        lax.psum(grad_up.astype(jnp.bfloat16), "ctx").astype(jnp.float32),
        lax.psum(grad_down.astype(jnp.bfloat16), "ctx").astype(jnp.float32),
    )


def solution(mesh):
    placed = (
        P(("ctx", "tp"), None),
        P(),
        P(None, "tp"),
        P(None, "tp"),
        P(None, "tp"),
        P("tp", None),
        P(None, "tp"),
        P(),
        P(),
        P(None, None, "tp"),
        P(None, None, "tp"),
        P(None, "tp", None),
        P(),
        P(),
        P(),
        P("ctx", None),
        P(("ctx", "tp"), None),
    )
    return jax.shard_map(
        on_device,
        mesh=mesh,
        in_specs=placed,
        out_specs=(
            P(("ctx", "tp"), None),
            P(("ctx", "tp"), None),
            P("tp"),
            P(None, "tp"),
            P(None, "tp"),
            P(None, "tp"),
            P("tp", None),
            P(None, "tp"),
            P("tp"),
            P("tp", None),
            P(None, None, "tp"),
            P(None, None, "tp"),
            P(None, "tp", None),
        ),
        check_vma=False,
    )
```

```python
import functools

import jax
import jax.numpy as jnp
from jax import lax
from jax.experimental import pallas as pl
from jax.experimental.pallas import tpu as pltpu
from jax.sharding import PartitionSpec as P

DH = 64
BLOCK = 128


EPS = 1e-06
NEG = -1e30
HIGH = lax.Precision.HIGHEST


LOG2E = 1.4426950408889634
KT = 512
VMEM_LIMIT = 56 * 1024 * 1024


def dot(left, right):
    return jnp.dot(left, right, preferred_element_type=jnp.float32)


def place_pairs(nat_ref, part_refs, k_row, count, keys_flat, keys_tall):
    keys_flat[:, :BLOCK] = jnp.zeros((2 * DH, BLOCK), keys_flat.dtype)
    keys_tall[:BLOCK, :] = jnp.zeros((BLOCK, 2 * DH), keys_tall.dtype)
    for part, ref in enumerate(part_refs):
        row = k_row if part == 0 else 0

        def one(index, _, part=part, ref=ref, row=row):
            at = pl.multiple_of((nat_ref[part * count + index] + 1) * BLOCK, BLOCK)
            pair = ref[index, row : row + 2 * DH, :]
            keys_flat[:, pl.ds(at, BLOCK)] = pair
            keys_tall[pl.ds(at, BLOCK), :] = pair.T
            return 0

        lax.fori_loop(0, count, one, 0)


def fill_near_bias(thr_ref, tab_ref, near_bias, bucket_count):
    key_ids = lax.broadcasted_iota(jnp.int32, (2 * BLOCK, BLOCK), 0)
    query_ids = lax.broadcasted_iota(jnp.int32, (2 * BLOCK, BLOCK), 1)
    distance = query_ids + BLOCK - key_ids
    value = jnp.full((2 * BLOCK, BLOCK), tab_ref[0], jnp.float32)
    for bucket in range(1, bucket_count):
        value = jnp.where(distance >= thr_ref[bucket], tab_ref[bucket], value)
    near_bias[...] = jnp.where(distance >= 0, value, NEG)


def pair_ids(nat_ref, tile, order_ref):
    slot_a = order_ref[2 * tile]
    slot_b = order_ref[2 * tile + 1]
    return slot_a, slot_b, nat_ref[slot_a], nat_ref[slot_b]


def lane_pair(first, second):
    return jnp.concatenate([first, second], axis=1)


def forward_kernel(
    bucket_count,
    parts,
    nat_ref,
    order_ref,
    low_ref,
    thr_ref,
    tab_ref,
    seq_ref,
    *rest,
):
    part_refs = rest[:parts]
    out_ref, full_ref, lse_ref = rest[parts : parts + 3]
    keys_flat, keys_tall, near_bias = rest[parts + 3 :]
    own_ref = part_refs[0]
    count = own_ref.shape[0]
    total = keys_tall.shape[0] - BLOCK
    scale = DH ** (-0.5) * LOG2E
    bf16 = jnp.bfloat16
    place_pairs(nat_ref, part_refs, DH, count, keys_flat, keys_tall)
    fill_near_bias(thr_ref, tab_ref, near_bias, bucket_count)
    near_ids = lax.broadcasted_iota(jnp.int32, (2 * BLOCK, BLOCK), 0)
    far_ids = lax.broadcasted_iota(jnp.int32, (KT, 2 * BLOCK), 0)

    def one_tile(tile, _):
        slot_a, slot_b, blk_a, blk_b = pair_ids(nat_ref, tile, order_ref)
        q_pair = lane_pair(own_ref[slot_a, :DH, :], own_ref[slot_b, :DH, :])
        q_wide = jnp.concatenate([q_pair, jnp.zeros_like(q_pair)], axis=0)
        starts = []
        stats = []
        for half, blk in enumerate((blk_a, blk_b)):
            at = pl.multiple_of(blk * BLOCK, BLOCK)
            start = seq_ref[pl.ds(blk, 1), :]
            starts.append(start)
            s = dot(
                keys_tall[pl.ds(at, 2 * BLOCK), :],
                q_wide[:, half * BLOCK : (half + 1) * BLOCK],
            )
            s = s * scale + near_bias[...]
            s = jnp.where(near_ids >= start - (blk - 1) * BLOCK, s, NEG)
            top = jnp.max(s, axis=0, keepdims=True)
            p = jnp.exp2(s - top)
            acc = dot(keys_flat[DH:, pl.ds(at, 2 * BLOCK)], p.astype(bf16))
            stats.append((top, jnp.sum(p, axis=0, keepdims=True), acc))
        top = lane_pair(stats[0][0], stats[1][0])
        norm = lane_pair(stats[0][1], stats[1][1])
        acc = lane_pair(stats[0][2], stats[1][2])
        start = lane_pair(*starts)
        lane = lax.broadcasted_iota(jnp.int32, (1, 2 * BLOCK), 1)
        stop = jnp.where(lane < BLOCK, (blk_a - 1) * BLOCK, (blk_b - 1) * BLOCK)
        first = low_ref[blk_a] * BLOCK
        steps = (jnp.maximum((blk_b - 1) * BLOCK - first, 0) + KT - 1) // KT

        def far(step, carry):
            top, norm, acc = carry
            begin = first + step * KT
            at = jnp.minimum(begin, total - KT)
            here = pl.multiple_of(at + BLOCK, BLOCK)
            s = dot(keys_tall[pl.ds(here, KT), :], q_wide)
            valid = (far_ids >= jnp.maximum(start, begin) - at) & (far_ids < stop - at)
            s = jnp.where(valid, s * scale, NEG)
            new_top = jnp.maximum(top, jnp.max(s, axis=0, keepdims=True))
            p = jnp.exp2(s - new_top)
            factor = jnp.exp2(top - new_top)
            norm = norm * factor + jnp.sum(p, axis=0, keepdims=True)
            acc = acc * factor + dot(keys_flat[DH:, pl.ds(here, KT)], p.astype(bf16))
            return new_top, norm, acc

        top, norm, acc = lax.fori_loop(0, steps, far, (top, norm, acc))
        result = acc / norm
        lse = top + jnp.log(norm) * LOG2E
        for half, slot in enumerate((slot_a, slot_b)):
            part = result[:, half * BLOCK : (half + 1) * BLOCK]
            full_ref[pl.ds(slot, 1)] = part[None]
            out_ref[pl.ds(slot, 1)] = part.astype(bf16)[None]
            lse_ref[pl.ds(slot, 1), :] = lse[:, half * BLOCK : (half + 1) * BLOCK]
        return 0

    lax.fori_loop(0, count // 2, one_tile, 0)


def backward_kernel(
    bucket_count,
    parts,
    nat_ref,
    order_ref,
    low_ref,
    thr_ref,
    tab_ref,
    seq_ref,
    *rest,
):
    part_refs = rest[:parts]
    dout_ref, full_ref, lse_ref = rest[parts : parts + 3]
    dq_ref = rest[parts + 3]
    dkv_refs = rest[parts + 4 : 2 * parts + 4]
    table_ref = rest[2 * parts + 4]
    keys_flat, keys_tall, near_bias, grads, near_grads = rest[2 * parts + 5 :]
    own_ref = part_refs[0]
    count = own_ref.shape[0]
    total = keys_tall.shape[0] - BLOCK
    scale = DH ** (-0.5) * LOG2E
    bf16 = jnp.bfloat16
    f32 = jnp.float32
    place_pairs(nat_ref, part_refs, DH, count, keys_flat, keys_tall)
    fill_near_bias(thr_ref, tab_ref, near_bias, bucket_count)
    grads[...] = jnp.zeros_like(grads)
    near_grads[...] = jnp.zeros_like(near_grads)
    near_ids = lax.broadcasted_iota(jnp.int32, (2 * BLOCK, BLOCK), 0)
    far_ids = lax.broadcasted_iota(jnp.int32, (KT, 2 * BLOCK), 0)
    low_lane = lax.broadcasted_iota(jnp.int32, (BLOCK, 2 * DH), 1) < DH

    def one_tile(tile, _):
        slot_a, slot_b, blk_a, blk_b = pair_ids(nat_ref, tile, order_ref)
        starts, lses, sums, rights, out_sides, q_sides, dq_near = [], [], [], [], [], [], []
        for slot, blk in ((slot_a, blk_a), (slot_b, blk_b)):
            at = pl.multiple_of(blk * BLOCK, BLOCK)
            start = seq_ref[pl.ds(blk, 1), :]
            q_t = own_ref[slot, :DH, :]
            do_t = dout_ref[slot]
            lse = lse_ref[pl.ds(slot, 1), :]
            dsum = jnp.sum(do_t.astype(f32) * full_ref[slot], axis=0, keepdims=True)
            zero = jnp.zeros_like(q_t)
            right = lane_pair(
                jnp.concatenate([q_t, zero], axis=0), jnp.concatenate([zero, do_t], axis=0)
            )
            both = jnp.concatenate([q_t, do_t], axis=0).T
            none = jnp.zeros_like(both)
            q_side = jnp.where(low_lane, both, none)
            out_side = jnp.where(low_lane, none, both)
            s_dp = dot(keys_tall[pl.ds(at, 2 * BLOCK), :], right)
            s = s_dp[:, :BLOCK] * scale + near_bias[...]
            s = jnp.where(near_ids >= start - (blk - 1) * BLOCK, s, NEG)
            p = jnp.exp2(s - lse)
            ds = (p * (s_dp[:, BLOCK:] - dsum)).astype(bf16)
            grads[pl.ds(at, 2 * BLOCK), :] += dot(
                lane_pair(p.astype(bf16), ds), jnp.concatenate([out_side, q_side], axis=0)
            )
            near_grads[...] += ds.astype(f32)
            dq_near.append(dot(keys_flat[:DH, pl.ds(at, 2 * BLOCK)], ds))
            starts.append(start)
            lses.append(lse)
            sums.append(dsum)
            rights.append(right)
            out_sides.append(out_side)
            q_sides.append(q_side)
        start = lane_pair(*starts)
        lse = lane_pair(*lses)
        dsum = lane_pair(*sums)
        right = jnp.concatenate(
            [
                rights[0][:, :BLOCK],
                rights[1][:, :BLOCK],
                rights[0][:, BLOCK:],
                rights[1][:, BLOCK:],
            ],
            axis=1,
        )
        sides = jnp.concatenate(out_sides + q_sides, axis=0)
        lane = lax.broadcasted_iota(jnp.int32, (1, 2 * BLOCK), 1)
        stop = jnp.where(lane < BLOCK, (blk_a - 1) * BLOCK, (blk_b - 1) * BLOCK)
        first = low_ref[blk_a] * BLOCK
        steps = (jnp.maximum((blk_b - 1) * BLOCK - first, 0) + KT - 1) // KT

        def far(step, dq):
            begin = first + step * KT
            at = jnp.minimum(begin, total - KT)
            here = pl.multiple_of(at + BLOCK, BLOCK)
            s_dp = dot(keys_tall[pl.ds(here, KT), :], right)
            valid = (far_ids >= jnp.maximum(start, begin) - at) & (far_ids < stop - at)
            s = jnp.where(valid, s_dp[:, : 2 * BLOCK] * scale, NEG)
            p = jnp.exp2(s - lse)
            ds = (p * (s_dp[:, 2 * BLOCK :] - dsum)).astype(bf16)
            grads[pl.ds(here, KT), :] += dot(lane_pair(p.astype(bf16), ds), sides)
            return dq + dot(keys_flat[:DH, pl.ds(here, KT)], ds)

        dq = lax.fori_loop(0, steps, far, lane_pair(*dq_near)) * DH ** (-0.5)
        for half, slot in enumerate((slot_a, slot_b)):
            part = dq[:, half * BLOCK : (half + 1) * BLOCK]
            dq_ref[pl.ds(slot, 1)] = part.astype(bf16)[None]
        return 0

    lax.fori_loop(0, count // 2, one_tile, 0)
    key_lane = jnp.where(low_lane, DH ** (-0.5), 1.0)
    for part in range(parts):

        def give(index, _, part=part):
            at = pl.multiple_of((nat_ref[part * count + index] + 1) * BLOCK, BLOCK)
            block = grads[pl.ds(at, BLOCK), :] * key_lane
            dkv_refs[part][pl.ds(index, 1)] = block.T.astype(bf16)[None]
            return 0

        lax.fori_loop(0, count, give, 0)
    key_ids = lax.broadcasted_iota(jnp.int32, (2 * BLOCK, BLOCK), 0)
    query_ids = lax.broadcasted_iota(jnp.int32, (2 * BLOCK, BLOCK), 1)
    distance = query_ids + BLOCK - key_ids
    near = near_grads[...]
    out_lane = lax.broadcasted_iota(jnp.int32, (1, BLOCK), 1)
    above = jnp.sum(near, axis=(0, 1), keepdims=True)
    result = jnp.zeros((1, BLOCK), f32)
    seen = jnp.zeros((1, 1), f32)
    for bucket in range(1, bucket_count):
        kept = jnp.sum(
            jnp.where(distance >= thr_ref[bucket], near, 0.0), axis=(0, 1), keepdims=True
        )
        result = jnp.where(out_lane == bucket - 1, above - kept, result)
        seen = seen + (above - kept)
        above = kept
    table_ref[...] = jnp.where(out_lane == bucket_count - 1, -seen, result)


def attention_call(kernel, parts, bucket_count, scalars, seq_start, arrays, out_shape, total, extra):
    smem = pl.BlockSpec(memory_space=pltpu.SMEM)
    team_size = parts
    vmem = pl.BlockSpec(memory_space=pltpu.VMEM)
    operands = list(scalars) + [seq_start] + list(arrays)
    scratch = [
        pltpu.VMEM((2 * DH, total + BLOCK), jnp.bfloat16),
        pltpu.VMEM((total + BLOCK, 2 * DH), jnp.bfloat16),
        pltpu.VMEM((2 * BLOCK, BLOCK), jnp.float32),
    ] + extra
    return pl.pallas_call(
        functools.partial(kernel, bucket_count, parts),
        out_shape=out_shape,
        in_specs=[smem] * len(scalars) + [vmem] * (1 + len(arrays)),
        out_specs=[vmem] * len(out_shape),
        scratch_shapes=scratch,
        compiler_params=pltpu.CompilerParams(vmem_limit_bytes=VMEM_LIMIT),
        cost_estimate=pl.CostEstimate(
            flops=total * total * DH * 8,
            bytes_accessed=total * DH * 400,
            transcendentals=total * total // (2 * team_size),
        ),
    )(*operands)


def turn_halves(x, axis, amounts, sign):
    halves = x.shape[axis + 1]
    shape = [1] * x.ndim
    shape[axis] = x.shape[axis]
    amounts = amounts.reshape(shape)
    result = x
    for step in range(1, halves):
        result = jnp.where(amounts == step, jnp.roll(x, -sign * step, axis=axis + 1), result)
    return result


GELU_A = 0.7978845608028654
GELU_B = 0.044715
ROWS = 512


def dot_nt(left, right):
    return lax.dot_general(
        left, right, (((1,), (1,)), ((), ())), preferred_element_type=jnp.float32
    )


def dot_tn(left, right):
    return lax.dot_general(
        left, right, (((0,), (0,)), ((), ())), preferred_element_type=jnp.float32
    )


def lane_of(column, shape):
    return lax.broadcasted_iota(jnp.int32, shape, 1) == column


def pad_units(weight, axis):
    extra = -weight.shape[axis] % (2 * BLOCK)
    pads = [(0, 0)] * weight.ndim
    pads[axis] = (0, extra)
    return jnp.pad(weight, pads)


def expert_kernel(
    experts,
    h_ref,
    router_ref,
    keep_ref,
    gate_ref,
    up_ref,
    back_ref,
    dh_ref,
    hidden_ref,
    dgate_ref,
    dup_ref,
    dlogits_ref,
    total,
    gates,
    dots,
):
    expert = pl.program_id(0)
    rows = pl.ds(pl.multiple_of(pl.program_id(1) * ROWS, ROWS), ROWS)
    f32 = jnp.float32
    bf16 = jnp.bfloat16
    lanes = (ROWS, router_ref.shape[1])
    h = h_ref[rows, :]

    @pl.when(expert == 0)
    def _():
        logits = dot(h, router_ref[...])
        real = lax.broadcasted_iota(jnp.int32, lanes, 1) < experts
        logits = jnp.where(real, logits, NEG)
        expo = jnp.exp(logits - jnp.max(logits, axis=1, keepdims=True))
        gates[rows, :] = expo / jnp.sum(expo, axis=1, keepdims=True)
        dots[rows, :] = jnp.zeros(lanes, f32)

    here = lane_of(expert, lanes)
    weight = jnp.sum(
        jnp.where(here, gates[rows, :] * keep_ref[rows, :], 0.0), axis=1, keepdims=True
    )
    g = dot_nt(h, gate_ref[0])
    u = dot_nt(h, up_ref[0])
    c = back_ref[0]
    square = g * g
    th = jnp.tanh(GELU_A * g * (1.0 + GELU_B * square))
    cdf = 0.5 + 0.5 * th
    gelu = g * cdf
    slope = cdf + (0.5 * GELU_A) * g * (1.0 - th * th) * (1.0 + 3.0 * GELU_B * square)
    hidden = (gelu * u).astype(bf16).astype(f32)
    hidden_ref[0] = (hidden * weight).astype(bf16)
    dots[rows, :] = jnp.where(here, jnp.sum(hidden * c, axis=1, keepdims=True), dots[rows, :])
    dc = c * weight
    dup = (dc * gelu).astype(bf16)
    dgate = (dc * u * slope).astype(bf16)
    dup_ref[0] = dup
    dgate_ref[0] = dgate
    part = dot(dgate, gate_ref[0]) + dot(dup, up_ref[0])

    @pl.when(expert == 0)
    def _():
        total[rows, :] = part

    @pl.when((expert > 0) & (expert < experts - 1))
    def _():
        total[rows, :] += part

    @pl.when(expert == experts - 1)
    def _():
        probs = gates[rows, :]
        dg = dots[rows, :] * keep_ref[rows, :]
        dl = probs * (dg - jnp.sum(probs * dg, axis=1, keepdims=True))
        dlogits_ref[rows, :] = dl
        high = dl.astype(bf16)
        rest = (dl - high.astype(f32)).astype(bf16)
        extra = dot_nt(high, router_ref[...]) + dot_nt(rest, router_ref[...])
        dh_ref[rows, :] = (total[rows, :] + part + extra).astype(bf16)


def expert_layer(h_all, router_wide, keep_wide, w_gate, w_up, back):
    experts, units, width = w_gate.shape
    rows = h_all.shape[0]
    lanes = router_wide.shape[1]
    f32 = jnp.float32
    bf16 = jnp.bfloat16
    whole = lambda e, c: (0, 0)
    weights = pl.BlockSpec((1, units, width), lambda e, c: (e, 0, 0))
    tile = pl.BlockSpec((1, ROWS, units), lambda e, c: (e, c, 0))
    wide = jax.ShapeDtypeStruct((experts, rows, units), bf16)
    return pl.pallas_call(
        functools.partial(expert_kernel, experts),
        out_shape=[
            jax.ShapeDtypeStruct((rows, width), bf16),
            wide,
            wide,
            wide,
            jax.ShapeDtypeStruct((rows, lanes), f32),
        ],
        grid=(experts, rows // ROWS),
        in_specs=[
            pl.BlockSpec((rows, width), whole),
            pl.BlockSpec((width, lanes), whole),
            pl.BlockSpec((rows, lanes), whole),
            weights,
            weights,
            tile,
        ],
        out_specs=[
            pl.BlockSpec((rows, width), whole),
            tile,
            tile,
            tile,
            pl.BlockSpec((rows, lanes), whole),
        ],
        scratch_shapes=[
            pltpu.VMEM((rows, width), f32),
            pltpu.VMEM((rows, lanes), f32),
            pltpu.VMEM((rows, lanes), f32),
        ],
        compiler_params=pltpu.CompilerParams(vmem_limit_bytes=VMEM_LIMIT),
        cost_estimate=pl.CostEstimate(
            flops=8 * experts * rows * units * width,
            bytes_accessed=experts * units * (4 * width + 10 * rows) + 4 * rows * width,
            transcendentals=experts * rows * units,
        ),
    )(h_all, router_wide, keep_wide, w_gate, w_up, back)


def weight_grads_kernel(first_ref, h_ref, grad_ref, hidden_ref, dgate_ref, dup_ref, *rest):
    outs = rest[-3:]
    lefts = (dgate_ref, dup_ref, hidden_ref)
    rights = (h_ref, h_ref, grad_ref)
    for index, (left, right, out) in enumerate(zip(lefts, rights, outs)):
        part = dot_tn(left[0], right[...])[: out.shape[1]]
        if len(rest) > 3:
            part = part + rest[index][0].astype(jnp.float32)
        out[0] = part.astype(out.dtype)


def weight_grads(first, count, real, h_all, grad_all, hidden, dgate, dup, arrived):
    _, rows, units = hidden.shape
    width = h_all.shape[1]
    whole = pl.BlockSpec((rows, width), lambda e, first: (0, 0))
    tile = pl.BlockSpec((1, rows, units), lambda e, first: (first[0] + e, 0, 0))
    out = pl.BlockSpec((1, real, width), lambda e, first: (e, 0, 0))
    return pl.pallas_call(
        weight_grads_kernel,
        out_shape=[jax.ShapeDtypeStruct((count, real, width), jnp.bfloat16)] * 3,
        grid_spec=pltpu.PrefetchScalarGridSpec(
            num_scalar_prefetch=1,
            grid=(count,),
            in_specs=[whole, whole, tile, tile, tile] + [out] * len(arrived),
            out_specs=[out] * 3,
        ),
        compiler_params=pltpu.CompilerParams(vmem_limit_bytes=VMEM_LIMIT),
        cost_estimate=pl.CostEstimate(
            flops=6 * count * rows * units * width,
            bytes_accessed=count * units * 6 * (rows + width) + 4 * rows * width,
            transcendentals=0,
        ),
    )(first, h_all, grad_all, hidden, dgate, dup, *arrived)


def kept_choices(group_routes, experts, capacity):
    count, top_count = group_routes.shape
    flat = group_routes.T.reshape(-1)
    hot = (flat[:, None] == jnp.arange(experts, dtype=jnp.int32)[None, :]).astype(jnp.int32)
    earlier = jnp.cumsum(hot, axis=0) - hot
    kept = jnp.where(earlier < capacity, hot, 0)
    return jnp.sum(kept.reshape(top_count, count, experts), axis=0).astype(jnp.float32)


def on_device(
    layer_in,
    gain_one,
    w_query,
    w_key,
    w_value,
    w_out,
    bias_table,
    gain_two,
    w_router,
    w_gate,
    w_up,
    w_down,
    lengths,
    block_perm,
    buckets,
    routes,
    cotangent,
):
    tp_count = lax.axis_size("tp")
    ctx_count = lax.axis_size("ctx")
    tp_index = lax.axis_index("tp")
    ctx_index = lax.axis_index("ctx")
    rows_dev = layer_in.shape[0]
    width = layer_in.shape[1]
    group_rows = rows_dev * tp_count
    width_loc = w_query.shape[1]
    head_count = width_loc // DH
    blocks_group = group_rows // BLOCK
    experts = w_gate.shape[0]
    top_count = routes.shape[1]
    capacity = 5 * top_count * group_rows // (4 * experts)
    units = w_gate.shape[2]
    core = ctx_index % 2
    bucket_count = bias_table.shape[0]
    f32 = jnp.float32
    bf16 = jnp.bfloat16
    x_float = layer_in.astype(f32)
    inv_one = lax.rsqrt(jnp.mean(x_float * x_float, axis=1, keepdims=True) + EPS)
    normed_one = x_float * inv_one
    h_one = (normed_one * gain_one).astype(bf16)
    h_one_all = lax.all_gather(h_one, "tp", axis=0, tiled=True)
    gate_wide = pad_units(jnp.swapaxes(w_gate, 1, 2), 1)
    up_wide = pad_units(jnp.swapaxes(w_up, 1, 2), 1)
    down_wide = pad_units(w_down, 1)
    h_one_all, w_out_own, cotangent_own, gate_wide, up_wide, down_wide = (
        lax.optimization_barrier(
            (h_one_all, w_out, cotangent, gate_wide, up_wide, down_wide)
        )
    )

    def turned(x, axis, step):
        size = lax.axis_size(axis)
        return lax.ppermute(x, axis, [(at, (at + step) % size) for at in range(size)])

    def crossed(x, axis, bits):
        size = lax.axis_size(axis)
        return lax.ppermute(x, axis, [(at, at ^ bits) for at in range(size)])

    def tp_scatter(x):
        chunks = x.reshape((tp_count, x.shape[0] // tp_count) + x.shape[1:])
        pieces = [lax.dynamic_index_in_dim(chunks, tp_index, 0, False)]
        for step in range(1, tp_count):
            chunk = lax.dynamic_index_in_dim(chunks, (tp_index + step) % tp_count, 0, False)
            pieces.append(turned(chunk, "tp", step))
        return pieces

    def summed(pieces):
        total = pieces[0].astype(f32)
        for piece in pieces[1:]:
            total = total + piece.astype(f32)
        return total

    chips = ctx_count // 2
    chip = ctx_index // 2

    def ctx_sum(x):
        half = x.shape[0] // 2
        away = lax.dynamic_slice_in_dim(x, (1 - core) * half, half, 0)
        mine = lax.dynamic_slice_in_dim(x, core * half, half, 0)
        mine = (mine.astype(f32) + crossed(away, "ctx", 1).astype(f32)).astype(bf16)
        chunks = mine.reshape((chips, half // chips) + x.shape[1:])
        total = lax.dynamic_index_in_dim(chunks, chip, 0, False).astype(f32)
        for bits in range(1, chips):
            chunk = lax.dynamic_index_in_dim(chunks, chip ^ bits, 0, False)
            total = total + crossed(chunk, "ctx", 2 * bits).astype(f32)
        total = total.astype(bf16)
        result = lax.dynamic_update_index_in_dim(jnp.zeros_like(chunks), total, chip, 0)
        for bits in range(1, chips):
            got = crossed(total, "ctx", 2 * bits)
            result = lax.dynamic_update_index_in_dim(result, got, chip ^ bits, 0)
        result = result.reshape((half,) + x.shape[1:])
        other = crossed(result, "ctx", 1)
        first = jnp.where(core == 0, result, other)
        second = jnp.where(core == 0, other, result)
        return jnp.concatenate([first, second], axis=0).astype(f32)

    def sum_everywhere(x):
        for axis in ("ctx", "tp"):
            bits = 1
            while bits < lax.axis_size(axis):
                x = x + crossed(x, axis, bits)
                bits *= 2
        return x

    w_out_all = lax.all_gather(w_out_own, "tp", axis=0, tiled=True)
    grad_all = lax.all_gather(cotangent_own, "tp", axis=0, tiled=True)
    w_qkv = jnp.concatenate([w_query, w_key, w_value], axis=1)
    qkv = lax.dot_general(
        w_qkv, h_one_all, (((0,), (1,)), ((), ())), preferred_element_type=f32
    ).astype(bf16)
    team = ctx_count // head_count
    member = ctx_index % team
    my_head = ctx_index // team
    pair_count = blocks_group // team
    slot_blocks = ctx_count * pair_count
    total = ctx_count * group_rows
    pair_ids_m = jnp.arange(pair_count, dtype=jnp.int32)
    turn = (ctx_index + pair_ids_m) % team
    ends = jnp.cumsum(lengths)
    begins = ends - lengths
    places = jnp.arange(total, dtype=jnp.int32)
    seq_start = jnp.max(
        jnp.where(begins[None, :] <= places[:, None], begins[None, :], 0), axis=1
    ).reshape(total // BLOCK, BLOCK)
    low_block = seq_start[:, 0] // BLOCK
    thresholds = jnp.sum(
        (buckets[None, :] < jnp.arange(bucket_count, dtype=jnp.int32)[:, None]).astype(jnp.int32),
        axis=1,
    )
    head_hot = (jnp.arange(head_count, dtype=jnp.int32) == my_head).astype(f32)
    my_table = jnp.sum(bias_table * head_hot[None, :], axis=1)
    near_table = (my_table - my_table[bucket_count - 1]) * LOG2E
    sources = jnp.arange(ctx_count, dtype=jnp.int32)
    members = (member + jnp.arange(team, dtype=jnp.int32)) % team
    half_of = (members[:, None, None] + sources[None, :, None] + pair_ids_m[None, None, :]) % team
    perm_pairs = block_perm.reshape(1, ctx_count, pair_count, team)
    natural = jnp.sum(
        jnp.where(
            half_of[..., None] == jnp.arange(team, dtype=jnp.int32)[None, None, None, :],
            perm_pairs,
            0,
        ),
        axis=3,
    ).reshape(-1)
    own_natural = natural[:slot_blocks]
    rank = jnp.sum((own_natural[None, :] < own_natural[:, None]).astype(jnp.int32), axis=1)
    slots = jnp.arange(slot_blocks, dtype=jnp.int32)
    order = jnp.sum(jnp.where(rank[None, :] == slots[:, None], slots[None, :], 0), axis=1)
    scalars = (natural, order, low_block, thresholds, near_table)

    def to_heads(x, kinds):
        split = x.reshape(kinds, head_count, DH, pair_count, team, BLOCK)
        split = turn_halves(split, 3, turn, 1)
        send = split.transpose(1, 4, 3, 0, 2, 5).reshape(
            ctx_count, pair_count, kinds * DH, BLOCK
        )
        got = lax.all_to_all(send, "ctx", 0, 0, tiled=True)
        return got.reshape(slot_blocks, kinds * DH, BLOCK)

    def from_heads(x, kinds):
        send = x.reshape(ctx_count, pair_count, kinds * DH, BLOCK)
        got = lax.all_to_all(send, "ctx", 0, 0, tiled=True)
        split = got.reshape(head_count, team, pair_count, kinds, DH, BLOCK)
        split = split.transpose(3, 0, 4, 2, 1, 5)
        split = turn_halves(split, 3, turn, -1)
        return split.reshape(kinds * head_count * DH, group_rows)

    def team_shift(x, step):
        route = []
        for device in range(ctx_count):
            base = device // team * team
            route.append((device, base + (device % team + step) % team))
        return lax.ppermute(x, "ctx", route)

    direct = pair_count == tp_count
    spot = (ctx_index + tp_index) % team

    def rows_from_heads(x):
        if direct:
            got = lax.all_to_all(x, ("ctx", "tp"), 0, 0, tiled=True)
            split = got.reshape(head_count, 1, team, tp_count, DH, BLOCK)
            split = turn_halves(split, 1, spot[None], -1)
            split = split.transpose(3, 0, 4, 1, 2, 5)
        else:
            split = from_heads(x, 1).reshape(width_loc, tp_count, rows_dev)
            split = lax.all_to_all(split.transpose(1, 0, 2), "tp", 0, 0, tiled=True)
        return split.reshape(tp_count * width_loc, rows_dev)

    def heads_from_rows(x):
        if direct:
            split = x.reshape(tp_count, head_count, DH, 1, team, BLOCK)
            split = split.transpose(1, 3, 4, 0, 2, 5)
            split = turn_halves(split, 1, spot[None], 1)
            send = split.reshape(ctx_count * tp_count, DH, BLOCK)
            return lax.all_to_all(send, ("ctx", "tp"), 0, 0, tiled=True)
        send = x.reshape(tp_count, width_loc, rows_dev)
        got = lax.all_to_all(send, "tp", 0, 0, tiled=True)
        return to_heads(got.transpose(1, 0, 2).reshape(width_loc, group_rows), 1)

    own_qkv = to_heads(qkv, 3)
    own_pairs = own_qkv[:, DH:, :]
    parts = [own_qkv] + [team_shift(own_pairs, -step) for step in range(1, team)]
    head_block = (slot_blocks, DH, BLOCK)
    att_slots, att_full, log_total = attention_call(
        forward_kernel,
        team,
        bucket_count,
        scalars,
        seq_start,
        parts,
        [
            jax.ShapeDtypeStruct(head_block, bf16),
            jax.ShapeDtypeStruct(head_block, f32),
            jax.ShapeDtypeStruct((slot_blocks, BLOCK), f32),
        ],
        total,
        [],
    )
    attended_rows = rows_from_heads(att_slots)
    mixed_in = x_float + lax.dot_general(
        attended_rows, w_out_all, (((0,), (0,)), ((), ())), preferred_element_type=f32
    )
    inv_two = lax.rsqrt(jnp.mean(mixed_in * mixed_in, axis=1, keepdims=True) + EPS)
    normed_two = mixed_in * inv_two
    h_two = (normed_two * gain_two).astype(bf16)
    h_two_all = lax.all_gather(h_two, "tp", axis=0, tiled=True)
    lanes = BLOCK
    keep = kept_choices(routes, experts, capacity)
    keep_wide = jnp.pad(keep, ((0, 0), (0, lanes - experts)))
    router_wide = jnp.pad(w_router, ((0, 0), (0, lanes - experts)))
    back = jnp.einsum("rd,efd->erf", grad_all, down_wide, preferred_element_type=f32)
    d_h_part, hidden, d_gate_bf, d_up_bf, d_logits = expert_layer(
        h_two_all, router_wide, keep_wide, gate_wide, up_wide, back
    )
    d_h_two = lax.psum_scatter(d_h_part, "tp", scatter_dimension=0, tiled=True).astype(f32)
    some = experts // 2
    operands = (h_two_all, grad_all, hidden, d_gate_bf, d_up_bf)
    away = weight_grads(
        ((1 - core) * some).astype(jnp.int32).reshape(1), some, units, *operands, ()
    )
    arrived = [crossed(grads, "ctx", 1) for grads in away]
    mine = weight_grads(
        (core * some).astype(jnp.int32).reshape(1), some, units, *operands, arrived
    )
    d_h_two, *_ = lax.optimization_barrier((d_h_two, *mine))
    same_core = [list(range(first, ctx_count, 2)) for first in range(2)]

    def both_halves(grads):
        other = crossed(grads, "ctx", 1)
        first = jnp.where(core == 0, grads, other)
        second = jnp.where(core == 0, other, grads)
        return jnp.concatenate([first, second], axis=0).astype(f32)

    mine = lax.psum(tuple(mine), "ctx", axis_index_groups=same_core)
    grad_float = cotangent.astype(f32)
    grad_router_part = lax.dot_general(
        h_two_all.astype(f32),
        d_logits[:, :experts],
        (((0,), (0,)), ((), ())),
        precision=HIGH,
        preferred_element_type=f32,
    )
    d_norm_two = d_h_two * gain_two
    grad_gain_two_part = jnp.sum(d_h_two * normed_two, axis=0)
    d_mixed = grad_float + inv_two * (
        d_norm_two - normed_two * jnp.mean(d_norm_two * normed_two, axis=1, keepdims=True)
    )
    d_attn = d_mixed.astype(bf16)
    d_attended = lax.dot_general(
        w_out_all, d_attn, (((1,), (1,)), ((), ())), preferred_element_type=f32
    ).astype(bf16)
    d_att_slots = heads_from_rows(d_attended)
    hidden, d_attn = lax.optimization_barrier((hidden, d_attn))
    mixed_part = jnp.einsum(
        "ecf,efd->cd", hidden[:, :, :units], w_down, preferred_element_type=f32
    )
    mixed_pieces = tp_scatter(mixed_part.astype(bf16))
    out_pieces = tp_scatter(
        jnp.dot(attended_rows, d_attn, preferred_element_type=f32).astype(bf16)
    )
    pair_block = jax.ShapeDtypeStruct((slot_blocks, 2 * DH, BLOCK), bf16)
    back_out = attention_call(
        backward_kernel,
        team,
        bucket_count,
        scalars,
        seq_start,
        parts + [d_att_slots, att_full, log_total],
        [jax.ShapeDtypeStruct(head_block, bf16)]
        + [pair_block] * team
        + [jax.ShapeDtypeStruct((1, BLOCK), f32)],
        total,
        [
            pltpu.VMEM((total + BLOCK, 2 * DH), f32),
            pltpu.VMEM((2 * BLOCK, BLOCK), f32),
        ],
    )
    mixed_pieces, out_pieces, back_out = lax.optimization_barrier(
        (mixed_pieces, out_pieces, tuple(back_out))
    )
    layer_out = mixed_in + summed(mixed_pieces)
    grad_out = summed(out_pieces)
    pair_grads = back_out[1].astype(f32)
    for step in range(1, team):
        pair_grads = pair_grads + team_shift(back_out[1 + step], step).astype(f32)
    d_cat = from_heads(jnp.concatenate([back_out[0], pair_grads.astype(bf16)], axis=1), 3)
    grad_qkv = jnp.einsum("rd,hr->dh", h_one_all, d_cat, preferred_element_type=f32)
    table_part = jnp.pad(
        back_out[1 + team][0, :bucket_count, None] * head_hot[None, :],
        ((0, 0), (0, (tp_count - 1) * head_count)),
    )
    table_part = jnp.roll(table_part, tp_index * head_count, axis=1)
    gain_one_part = jnp.sum(grad_qkv * w_qkv.astype(f32), axis=1) / gain_one
    d_h_one_part = jnp.einsum("hr,dh->rd", d_cat, w_qkv, preferred_element_type=f32)
    d_h_one = lax.psum_scatter(
        d_h_one_part.astype(bf16), "tp", scatter_dimension=0, tiled=True
    ).astype(f32)
    d_norm_one = d_h_one * gain_one
    grad_x = d_mixed + inv_one * (
        d_norm_one - normed_one * jnp.mean(d_norm_one * normed_one, axis=1, keepdims=True)
    )
    small = jnp.concatenate(
        [
            gain_one_part,
            grad_gain_two_part,
            grad_router_part.reshape(-1),
            table_part.reshape(-1),
        ]
    )
    small = sum_everywhere(small.reshape(-1, BLOCK)).reshape(-1)
    own = width // tp_count
    gain_one_all, gain_two_all, router_all, table_all = jnp.split(
        small, [width, 2 * width, (2 + experts) * width]
    )
    gain_one_grad = lax.dynamic_slice_in_dim(gain_one_all, tp_index * own, own, 0)
    gain_two_grad = lax.dynamic_slice_in_dim(gain_two_all, tp_index * own, own, 0)
    router_grad = lax.dynamic_slice_in_dim(
        router_all.reshape(width, experts), tp_index * own, own, 0
    )
    table_grad = lax.dynamic_slice_in_dim(
        table_all.reshape(bucket_count, -1), tp_index * head_count, head_count, 1
    )
    grad_qkv, mine = lax.optimization_barrier((grad_qkv, mine))
    out_wide = grad_out.reshape(width, width_loc)
    wide = jnp.concatenate([grad_qkv, out_wide], axis=1)
    wide = ctx_sum(wide.astype(bf16))
    grad_qkv = wide[:, : 3 * width_loc]
    grad_out = wide[:, 3 * width_loc :].reshape(width_loc, width)
    grad_gate, grad_up, grad_down = [both_halves(grads) for grads in mine]
    return (
        layer_out,
        grad_x,
        gain_one_grad,
        grad_qkv[:, :width_loc],
        grad_qkv[:, width_loc : 2 * width_loc],
        grad_qkv[:, 2 * width_loc :],
        grad_out,
        table_grad,
        gain_two_grad,
        router_grad,
        jnp.swapaxes(grad_gate, 1, 2),
        jnp.swapaxes(grad_up, 1, 2),
        grad_down,
    )


def solution(mesh):
    placed = (
        P(("ctx", "tp"), None),
        P(),
        P(None, "tp"),
        P(None, "tp"),
        P(None, "tp"),
        P("tp", None),
        P(None, "tp"),
        P(),
        P(),
        P(None, None, "tp"),
        P(None, None, "tp"),
        P(None, "tp", None),
        P(),
        P(),
        P(),
        P("ctx", None),
        P(("ctx", "tp"), None),
    )
    return jax.shard_map(
        on_device,
        mesh=mesh,
        in_specs=placed,
        out_specs=(
            P(("ctx", "tp"), None),
            P(("ctx", "tp"), None),
            P("tp"),
            P(None, "tp"),
            P(None, "tp"),
            P(None, "tp"),
            P("tp", None),
            P(None, "tp"),
            P("tp"),
            P("tp", None),
            P(None, None, "tp"),
            P(None, None, "tp"),
            P(None, "tp", None),
        ),
        check_vma=False,
    )
```

```python
import functools

import jax
import jax.numpy as jnp
from jax import lax
from jax.experimental import pallas as pl
from jax.experimental.pallas import tpu as pltpu
from jax.sharding import PartitionSpec as P

DH = 64
BLOCK = 128


EPS = 1e-06
NEG = -1e30
HIGH = lax.Precision.HIGHEST


LOG2E = 1.4426950408889634
KT = 512
GROUPS = 2
BACK_COST = 2
VMEM_LIMIT = 56 * 1024 * 1024


def dot(left, right):
    return jnp.dot(left, right, preferred_element_type=jnp.float32)


def place_pairs(nat_ref, part_refs, k_row, count, keys_flat, keys_tall):
    keys_flat[:, :BLOCK] = jnp.zeros((2 * DH, BLOCK), keys_flat.dtype)
    keys_tall[:BLOCK, :] = jnp.zeros((BLOCK, 2 * DH), keys_tall.dtype)
    for part, ref in enumerate(part_refs):
        row = k_row if part == 0 else 0

        def one(index, _, part=part, ref=ref, row=row):
            at = pl.multiple_of((nat_ref[part * count + index] + 1) * BLOCK, BLOCK)
            pair = ref[index, row : row + 2 * DH, :]
            keys_flat[:, pl.ds(at, BLOCK)] = pair
            keys_tall[pl.ds(at, BLOCK), :] = pair.T
            return 0

        lax.fori_loop(0, count, one, 0, unroll=8)


def fill_near_bias(thr_ref, tab_ref, near_bias, bucket_count):
    key_ids = lax.broadcasted_iota(jnp.int32, (2 * BLOCK, BLOCK), 0)
    query_ids = lax.broadcasted_iota(jnp.int32, (2 * BLOCK, BLOCK), 1)
    distance = query_ids + BLOCK - key_ids
    value = jnp.full((2 * BLOCK, BLOCK), tab_ref[0], jnp.float32)
    for bucket in range(1, bucket_count):
        value = jnp.where(distance >= thr_ref[bucket], tab_ref[bucket], value)
    near_bias[...] = jnp.where(distance >= 0, value, NEG)


def lane_pair(first, second):
    return jnp.concatenate([first, second], axis=1)


def tile_group(nat_ref, order_ref, low_ref, high_ref, index):
    slots = (order_ref[2 * index], order_ref[2 * index + 1])
    blocks = (nat_ref[slots[0]], nat_ref[slots[1]])
    lane = lax.broadcasted_iota(jnp.int32, (1, 2 * BLOCK), 1)
    stop = jnp.where(lane < BLOCK, (blocks[0] - 1) * BLOCK, (blocks[1] - 1) * BLOCK)
    first = low_ref[blocks[0]] * BLOCK
    steps = (jnp.maximum((blocks[1] - 1) * BLOCK - first, 0) + KT - 1) // KT
    return slots, blocks, stop, first, steps, high_ref[blocks[1]], (blocks[0] - 1) * BLOCK


def far_place(group, step, total):
    begin = group[3] + step * KT
    at = jnp.minimum(begin, total - KT)
    return begin, at, pl.multiple_of(at + BLOCK, BLOCK)


def all_inside(groups, step):
    inside = True
    for group in groups:
        begin = group[3] + step * KT
        inside = inside & (begin >= group[5]) & (begin + KT <= group[6])
    return inside


def far_valid(far_ids, group, start, begin, at):
    return (far_ids >= jnp.maximum(start, begin) - at) & (far_ids < group[2] - at)


def forward_kernel(
    bucket_count,
    parts,
    nat_ref,
    order_ref,
    low_ref,
    high_ref,
    thr_ref,
    tab_ref,
    seq_ref,
    *rest,
):
    part_refs = rest[:parts]
    out_ref, full_ref, lse_ref = rest[parts : parts + 3]
    keys_flat, keys_tall, near_bias = rest[parts + 3 :]
    own_ref = part_refs[0]
    count = own_ref.shape[0]
    total = keys_tall.shape[0] - BLOCK
    scale = DH ** (-0.5) * LOG2E
    bf16 = jnp.bfloat16
    place_pairs(nat_ref, part_refs, DH, count, keys_flat, keys_tall)
    fill_near_bias(thr_ref, tab_ref, near_bias, bucket_count)
    near_ids = lax.broadcasted_iota(jnp.int32, (2 * BLOCK, BLOCK), 0)
    far_ids = lax.broadcasted_iota(jnp.int32, (KT, 2 * BLOCK), 0)

    def one_tile(tile, _):
        groups = [
            tile_group(nat_ref, order_ref, low_ref, high_ref, GROUPS * tile + index)
            for index in range(GROUPS)
        ]
        queries, starts, init = [], [], []
        for slots, blocks, *_ in groups:
            q_pair = lane_pair(own_ref[slots[0], :DH, :], own_ref[slots[1], :DH, :])
            q_wide = jnp.concatenate([q_pair, jnp.zeros_like(q_pair)], axis=0)
            sides = []
            for half, blk in enumerate(blocks):
                at = pl.multiple_of(blk * BLOCK, BLOCK)
                start = seq_ref[pl.ds(blk, 1), :]
                s = dot(
                    keys_tall[pl.ds(at, 2 * BLOCK), :],
                    q_wide[:, half * BLOCK : (half + 1) * BLOCK],
                )
                s = s * scale + near_bias[...]
                s = jnp.where(near_ids >= start - (blk - 1) * BLOCK, s, NEG)
                top = jnp.max(s, axis=0, keepdims=True)
                p = jnp.exp2(s - top)
                acc = dot(keys_flat[DH:, pl.ds(at, 2 * BLOCK)], p.astype(bf16))
                sides.append((start, top, jnp.sum(p, axis=0, keepdims=True), acc))
            start, *stats = [lane_pair(x, y) for x, y in zip(*sides)]
            queries.append(q_wide)
            starts.append(start)
            init.append(tuple(stats))

        def update(step, carry, masked):
            places = [far_place(group, step, total) for group in groups]
            scores = [
                dot(keys_tall[pl.ds(here, KT), :], q_wide)
                for (_, _, here), q_wide in zip(places, queries)
            ]
            middle = []
            for index, (top, norm, acc) in enumerate(carry):
                begin, at, here = places[index]
                s = scores[index] * scale
                if masked:
                    valid = far_valid(far_ids, groups[index], starts[index], begin, at)
                    s = jnp.where(valid, s, NEG)
                new_top = jnp.maximum(top, jnp.max(s, axis=0, keepdims=True))
                p = jnp.exp2(s - new_top)
                factor = jnp.exp2(top - new_top)
                norm = norm * factor + jnp.sum(p, axis=0, keepdims=True)
                middle.append((new_top, norm, acc * factor, p.astype(bf16)))
            return tuple(
                (top, norm, acc + dot(keys_flat[DH:, pl.ds(here, KT)], p))
                for (top, norm, acc, p), (_, _, here) in zip(middle, places)
            )

        def far(step, carry):
            return lax.cond(
                all_inside(groups, step),
                lambda inner: update(step, inner, False),
                lambda inner: update(step, inner, True),
                carry,
            )

        steps = functools.reduce(jnp.maximum, [group[4] for group in groups])
        final = lax.fori_loop(0, steps, far, tuple(init))
        for (slots, *_), (top, norm, acc) in zip(groups, final):
            result = acc / norm
            lse = top + jnp.log(norm) * LOG2E
            for half, slot in enumerate(slots):
                part = result[:, half * BLOCK : (half + 1) * BLOCK]
                full_ref[pl.ds(slot, 1)] = part[None]
                out_ref[pl.ds(slot, 1)] = part.astype(bf16)[None]
                lse_ref[pl.ds(slot, 1), :] = lse[:, half * BLOCK : (half + 1) * BLOCK]
        return 0

    lax.fori_loop(0, count // (2 * GROUPS), one_tile, 0)


def backward_kernel(
    bucket_count,
    parts,
    nat_ref,
    order_ref,
    low_ref,
    high_ref,
    thr_ref,
    tab_ref,
    seq_ref,
    *rest,
):
    part_refs = rest[:parts]
    dout_ref, full_ref, lse_ref = rest[parts : parts + 3]
    dq_ref = rest[parts + 3]
    dkv_refs = rest[parts + 4 : 2 * parts + 4]
    table_ref = rest[2 * parts + 4]
    keys_flat, keys_tall, near_bias, grads, near_grads = rest[2 * parts + 5 :]
    own_ref = part_refs[0]
    count = own_ref.shape[0]
    total = keys_tall.shape[0] - BLOCK
    scale = DH ** (-0.5) * LOG2E
    bf16 = jnp.bfloat16
    f32 = jnp.float32
    place_pairs(nat_ref, part_refs, DH, count, keys_flat, keys_tall)
    fill_near_bias(thr_ref, tab_ref, near_bias, bucket_count)
    grads[...] = jnp.zeros_like(grads)
    near_grads[...] = jnp.zeros_like(near_grads)
    near_ids = lax.broadcasted_iota(jnp.int32, (2 * BLOCK, BLOCK), 0)
    far_ids = lax.broadcasted_iota(jnp.int32, (KT, 2 * BLOCK), 0)
    low_lane = lax.broadcasted_iota(jnp.int32, (BLOCK, 2 * DH), 1) < DH

    def one_tile(tile, _):
        groups = [
            tile_group(nat_ref, order_ref, low_ref, high_ref, GROUPS * tile + index)
            for index in range(GROUPS)
        ]
        fixed, init = [], []
        for slots, blocks, *_ in groups:
            sides = []
            for slot, blk in zip(slots, blocks):
                at = pl.multiple_of(blk * BLOCK, BLOCK)
                start = seq_ref[pl.ds(blk, 1), :]
                q_t = own_ref[slot, :DH, :]
                do_t = dout_ref[slot]
                lse = lse_ref[pl.ds(slot, 1), :]
                dsum = jnp.sum(do_t.astype(f32) * full_ref[slot], axis=0, keepdims=True)
                zero = jnp.zeros_like(q_t)
                q_wide = jnp.concatenate([q_t, zero], axis=0)
                do_wide = jnp.concatenate([zero, do_t], axis=0)
                both = jnp.concatenate([q_t, do_t], axis=0).T
                none = jnp.zeros_like(both)
                q_side = jnp.where(low_lane, both, none)
                out_side = jnp.where(low_lane, none, both)
                s_dp = dot(keys_tall[pl.ds(at, 2 * BLOCK), :], lane_pair(q_wide, do_wide))
                s = s_dp[:, :BLOCK] * scale + near_bias[...]
                s = jnp.where(near_ids >= start - (blk - 1) * BLOCK, s, NEG)
                p = jnp.exp2(s - lse)
                ds = (p * (s_dp[:, BLOCK:] - dsum)).astype(bf16)
                grads[pl.ds(at, 2 * BLOCK), :] += dot(
                    lane_pair(p.astype(bf16), ds),
                    jnp.concatenate([out_side, q_side], axis=0),
                )
                near_grads[...] += ds.astype(f32)
                dq = dot(keys_flat[:DH, pl.ds(at, 2 * BLOCK)], ds)
                sides.append((start, lse, dsum, q_wide, do_wide, dq, out_side, q_side))
            wide = [lane_pair(x, y) for x, y in zip(*[side[:6] for side in sides])]
            start, lse, dsum, q_wide, do_wide, dq = wide
            right = lane_pair(q_wide, do_wide)
            tall = jnp.concatenate(
                [sides[0][6], sides[1][6], sides[0][7], sides[1][7]], axis=0
            )
            fixed.append((start, lse, dsum, right, tall))
            init.append(dq)

        def update(step, carry, masked):
            places = [far_place(group, step, total) for group in groups]
            products = [
                dot(keys_tall[pl.ds(here, KT), :], right)
                for (_, _, here), (_, _, _, right, _) in zip(places, fixed)
            ]
            middle = []
            for index, (start, lse, dsum, _, _) in enumerate(fixed):
                begin, at, _ = places[index]
                s = products[index][:, : 2 * BLOCK] * scale
                if masked:
                    valid = far_valid(far_ids, groups[index], start, begin, at)
                    s = jnp.where(valid, s, NEG)
                p = jnp.exp2(s - lse)
                ds = (p * (products[index][:, 2 * BLOCK :] - dsum)).astype(bf16)
                middle.append((p.astype(bf16), ds))
            result = []
            for (p, ds), (_, _, here), (*_, tall), dq in zip(middle, places, fixed, carry):
                grads[pl.ds(here, KT), :] += dot(lane_pair(p, ds), tall)
                result.append(dq + dot(keys_flat[:DH, pl.ds(here, KT)], ds))
            return tuple(result)

        def far(step, carry):
            return lax.cond(
                all_inside(groups, step),
                lambda inner: update(step, inner, False),
                lambda inner: update(step, inner, True),
                carry,
            )

        steps = functools.reduce(jnp.maximum, [group[4] for group in groups])
        final = lax.fori_loop(0, steps, far, tuple(init))
        for (slots, *_), dq in zip(groups, final):
            dq = dq * DH ** (-0.5)
            for half, slot in enumerate(slots):
                part = dq[:, half * BLOCK : (half + 1) * BLOCK]
                dq_ref[pl.ds(slot, 1)] = part.astype(bf16)[None]
        return 0

    lax.fori_loop(0, count // (2 * GROUPS), one_tile, 0)
    key_lane = jnp.where(low_lane, DH ** (-0.5), 1.0)
    for part in range(parts):

        def give(index, _, part=part):
            at = pl.multiple_of((nat_ref[part * count + index] + 1) * BLOCK, BLOCK)
            block = grads[pl.ds(at, BLOCK), :] * key_lane
            dkv_refs[part][pl.ds(index, 1)] = block.T.astype(bf16)[None]
            return 0

        lax.fori_loop(0, count, give, 0, unroll=8)
    key_ids = lax.broadcasted_iota(jnp.int32, (2 * BLOCK, BLOCK), 0)
    query_ids = lax.broadcasted_iota(jnp.int32, (2 * BLOCK, BLOCK), 1)
    distance = query_ids + BLOCK - key_ids
    near = near_grads[...]
    out_lane = lax.broadcasted_iota(jnp.int32, (1, BLOCK), 1)
    above = jnp.sum(near, axis=(0, 1), keepdims=True)
    result = jnp.zeros((1, BLOCK), f32)
    seen = jnp.zeros((1, 1), f32)
    for bucket in range(1, bucket_count):
        kept = jnp.sum(
            jnp.where(distance >= thr_ref[bucket], near, 0.0), axis=(0, 1), keepdims=True
        )
        result = jnp.where(out_lane == bucket - 1, above - kept, result)
        seen = seen + (above - kept)
        above = kept
    table_ref[...] = jnp.where(out_lane == bucket_count - 1, -seen, result)


def attention_call(kernel, parts, bucket_count, scalars, seq_start, arrays, out_shape, total, extra, cost):
    smem = pl.BlockSpec(memory_space=pltpu.SMEM)
    team_size = parts
    vmem = pl.BlockSpec(memory_space=pltpu.VMEM)
    operands = list(scalars) + [seq_start] + list(arrays)
    scratch = [
        pltpu.VMEM((2 * DH, total + BLOCK), jnp.bfloat16),
        pltpu.VMEM((total + BLOCK, 2 * DH), jnp.bfloat16),
        pltpu.VMEM((2 * BLOCK, BLOCK), jnp.float32),
    ] + extra
    return pl.pallas_call(
        functools.partial(kernel, bucket_count, parts),
        out_shape=out_shape,
        in_specs=[smem] * len(scalars) + [vmem] * (1 + len(arrays)),
        out_specs=[vmem] * len(out_shape),
        scratch_shapes=scratch,
        compiler_params=pltpu.CompilerParams(vmem_limit_bytes=VMEM_LIMIT),
        cost_estimate=pl.CostEstimate(
            flops=total * total * DH * cost,
            bytes_accessed=total * DH * 50 * cost,
            transcendentals=0,
        ),
    )(*operands)


def turn_halves(x, axis, amounts, sign):
    halves = x.shape[axis + 1]
    shape = [1] * x.ndim
    shape[axis] = x.shape[axis]
    amounts = amounts.reshape(shape)
    result = x
    for step in range(1, halves):
        result = jnp.where(amounts == step, jnp.roll(x, -sign * step, axis=axis + 1), result)
    return result


GELU_A = 0.7978845608028654
GELU_B = 0.044715
ROWS = 512


def dot_nt(left, right):
    return lax.dot_general(
        left, right, (((1,), (1,)), ((), ())), preferred_element_type=jnp.float32
    )


def dot_tn(left, right):
    return lax.dot_general(
        left, right, (((0,), (0,)), ((), ())), preferred_element_type=jnp.float32
    )


def lane_of(column, shape):
    return lax.broadcasted_iota(jnp.int32, shape, 1) == column


def project_kernel(turn_ref, h_ref, query_ref, key_ref, value_ref, out_ref):
    heads, team = out_ref.shape[:2]
    turn = turn_ref[pl.program_id(0)]
    h = h_ref[...]
    for kind, weight in enumerate((query_ref, key_ref, value_ref)):
        flat = dot(h, weight[...]).T.astype(out_ref.dtype)
        rows = slice(kind * DH, (kind + 1) * DH)
        for half in range(team):
            member = lax.rem(half - turn + team, team)
            columns = flat[:, half * BLOCK : (half + 1) * BLOCK]
            for head in range(heads):
                block = columns[head * DH : (head + 1) * DH]
                out_ref[head, pl.ds(member, 1), 0, rows, :] = block[None]


def project(turn, h_all, weights, heads, team):
    rows, width = h_all.shape
    pairs = rows // (team * BLOCK)
    local = weights[0].shape[1]
    weight = pl.BlockSpec((width, local), lambda m, turn: (0, 0))
    return pl.pallas_call(
        project_kernel,
        out_shape=jax.ShapeDtypeStruct((heads, team, pairs, 3 * DH, BLOCK), jnp.bfloat16),
        grid_spec=pltpu.PrefetchScalarGridSpec(
            num_scalar_prefetch=1,
            grid=(pairs,),
            in_specs=[pl.BlockSpec((team * BLOCK, width), lambda m, turn: (m, 0))]
            + [weight] * 3,
            out_specs=pl.BlockSpec(
                (heads, team, 1, 3 * DH, BLOCK), lambda m, turn: (0, 0, m, 0, 0)
            ),
        ),
        compiler_params=pltpu.CompilerParams(vmem_limit_bytes=VMEM_LIMIT),
        cost_estimate=pl.CostEstimate(
            flops=6 * rows * width * local,
            bytes_accessed=2 * rows * (width + 3 * local) + 6 * width * local,
            transcendentals=0,
        ),
    )(turn, h_all, *weights)


def unproject_kernel(
    turn_ref,
    got_ref,
    h_ref,
    query_ref,
    key_ref,
    value_ref,
    out_ref,
    small_ref,
    gain_ref,
    dh_ref,
    wide_ref,
    total,
):
    heads, team = got_ref.shape[:2]
    local = query_ref.shape[1]
    step = pl.program_id(0)
    turn = turn_ref[step]
    h = h_ref[...]

    @pl.when(step == 0)
    def _():
        total[...] = jnp.zeros_like(total)

    dh = jnp.zeros(dh_ref.shape, jnp.float32)
    for kind, weight in enumerate((query_ref, key_ref, value_ref)):
        halves = []
        for half in range(team):
            member = lax.rem(half - turn + team, team)
            blocks = [
                got_ref[head, pl.ds(member, 1), 0, kind * DH : (kind + 1) * DH, :][0]
                for head in range(heads)
            ]
            halves.append(jnp.concatenate(blocks, axis=0))
        flat = jnp.concatenate(halves, axis=1)
        dh = dh + dot_nt(flat.T, weight[...])
        total[kind * local : (kind + 1) * local, :] += dot(flat, h)
    dh_ref[...] = dh.astype(dh_ref.dtype)

    @pl.when(step == pl.num_programs(0) - 1)
    def _():
        gain = jnp.zeros(gain_ref.shape, jnp.float32)
        for kind, weight in enumerate((query_ref, key_ref, value_ref)):
            rows = slice(kind * local, (kind + 1) * local)
            part = total[rows, :]
            wide_ref[rows, :] = part.astype(wide_ref.dtype)
            tall = weight[...].T.astype(jnp.float32)
            gain = gain + jnp.sum(part * tall, axis=0, keepdims=True)
        wide_ref[3 * local : 4 * local, :] = out_ref[...]
        row_ids = lax.broadcasted_iota(jnp.int32, small_ref.shape, 0)
        small = jnp.where(row_ids == 0, gain / gain_ref[...], small_ref[...])
        wide_ref[4 * local :, :] = small.astype(wide_ref.dtype)


def unproject(turn, got, h_all, weights, grad_out, small, gain):
    heads, team, pairs = got.shape[:3]
    rows, width = h_all.shape
    local = weights[0].shape[1]
    wide_rows = 4 * local + small.shape[0]
    block = pl.BlockSpec((team * BLOCK, width), lambda m, turn: (m, 0))
    whole = lambda m, turn: (0, 0)
    return pl.pallas_call(
        unproject_kernel,
        out_shape=[
            jax.ShapeDtypeStruct((rows, width), jnp.bfloat16),
            jax.ShapeDtypeStruct((wide_rows, width), jnp.bfloat16),
        ],
        grid_spec=pltpu.PrefetchScalarGridSpec(
            num_scalar_prefetch=1,
            grid=(pairs,),
            in_specs=[
                pl.BlockSpec(
                    (heads, team, 1, 3 * DH, BLOCK), lambda m, turn: (0, 0, m, 0, 0)
                ),
                block,
            ]
            + [pl.BlockSpec((width, local), whole)] * 3
            + [
                pl.BlockSpec((local, width), whole),
                pl.BlockSpec(small.shape, whole),
                pl.BlockSpec((1, width), whole),
            ],
            out_specs=[block, pl.BlockSpec((wide_rows, width), whole)],
            scratch_shapes=[pltpu.VMEM((3 * local, width), jnp.float32)],
        ),
        compiler_params=pltpu.CompilerParams(vmem_limit_bytes=VMEM_LIMIT),
        cost_estimate=pl.CostEstimate(
            flops=12 * rows * width * local,
            bytes_accessed=2 * rows * (2 * width + 3 * local) + 12 * width * local,
            transcendentals=0,
        ),
    )(turn, got, h_all, *weights, grad_out, small, gain)


def place_kernel(count, first_ref, *refs):
    for source, target in zip(refs[:count], refs[-count:]):
        target[...] = source[...].astype(target.dtype)


def place_half(first, halves, targets):
    some, units, width = halves[0].shape
    count = len(halves)
    source = pl.BlockSpec((1, units, width), lambda e, first: (e, 0, 0))
    target = pl.BlockSpec((1, units, width), lambda e, first: (first[0] + e, 0, 0))
    passed = [pl.BlockSpec(memory_space=pl.ANY)] * len(targets)
    return pl.pallas_call(
        functools.partial(place_kernel, count),
        out_shape=[jax.ShapeDtypeStruct((2 * some, units, width), jnp.float32)] * count,
        grid_spec=pltpu.PrefetchScalarGridSpec(
            num_scalar_prefetch=1,
            grid=(some,),
            in_specs=[source] * count + passed,
            out_specs=[target] * count,
        ),
        input_output_aliases={1 + count + at: at for at in range(len(targets))},
        compiler_params=pltpu.CompilerParams(vmem_limit_bytes=VMEM_LIMIT),
        cost_estimate=pl.CostEstimate(
            flops=0, bytes_accessed=6 * count * halves[0].size, transcendentals=0
        ),
    )(first, *halves, *targets)


def pad_units(weight, axis):
    extra = -weight.shape[axis] % (2 * BLOCK)
    pads = [(0, 0)] * weight.ndim
    pads[axis] = (0, extra)
    return jnp.pad(weight, pads)


def expert_kernel(
    experts,
    h_ref,
    router_ref,
    keep_ref,
    gate_ref,
    up_ref,
    back_ref,
    *rest,
):
    dh_ref, hidden_ref, dgate_ref, dup_ref, drouter_ref, total, gates, dots = rest[-8:]
    expert = pl.program_id(0)
    rows = slice(0, ROWS)
    f32 = jnp.float32
    bf16 = jnp.bfloat16
    lanes = (ROWS, router_ref.shape[1])
    h = h_ref[rows, :]

    @pl.when(expert == 0)
    def _():
        logits = dot(h, router_ref[...])
        real = lax.broadcasted_iota(jnp.int32, lanes, 1) < experts
        logits = jnp.where(real, logits, NEG)
        expo = jnp.exp(logits - jnp.max(logits, axis=1, keepdims=True))
        gates[rows, :] = expo / jnp.sum(expo, axis=1, keepdims=True)
        dots[rows, :] = jnp.zeros(lanes, f32)

    here = lane_of(expert, lanes)
    weight = jnp.sum(
        jnp.where(here, gates[rows, :] * keep_ref[rows, :], 0.0), axis=1, keepdims=True
    )
    g = dot_nt(h, gate_ref[0])
    u = dot_nt(h, up_ref[0])
    c = back_ref[0]
    square = g * g
    th = jnp.tanh(GELU_A * g * (1.0 + GELU_B * square))
    cdf = 0.5 + 0.5 * th
    gelu = g * cdf
    slope = cdf + (0.5 * GELU_A) * g * (1.0 - th * th) * (1.0 + 3.0 * GELU_B * square)
    hidden = (gelu * u).astype(bf16).astype(f32)
    hidden_ref[0] = (hidden * weight).astype(bf16)
    dots[rows, :] = jnp.where(here, jnp.sum(hidden * c, axis=1, keepdims=True), dots[rows, :])
    dc = c * weight
    dup = (dc * gelu).astype(bf16)
    dgate = (dc * u * slope).astype(bf16)
    dup_ref[0] = dup
    dgate_ref[0] = dgate
    part = dot(dgate, gate_ref[0]) + dot(dup, up_ref[0])

    @pl.when(expert == 0)
    def _():
        total[rows, :] = part

    @pl.when((expert > 0) & (expert < experts - 1))
    def _():
        total[rows, :] += part

    @pl.when(expert == experts - 1)
    def _():
        probs = gates[rows, :]
        dg = dots[rows, :] * keep_ref[rows, :]
        dl = probs * (dg - jnp.sum(probs * dg, axis=1, keepdims=True))
        high = dl.astype(bf16)
        low = (dl - high.astype(f32)).astype(bf16)
        drouter = dot_tn(high, h) + dot_tn(low, h)
        drouter_ref[...] = drouter[: drouter_ref.shape[0]]
        extra = dot_nt(high, router_ref[...]) + dot_nt(low, router_ref[...])
        dh_ref[rows, :] = (total[rows, :] + part + extra).astype(bf16)


def expert_layer(part, h_part, router_wide, keep_wide, w_gate, w_up, back, filled):
    experts, units, width = w_gate.shape
    rows = back.shape[1]
    lanes = router_wide.shape[1]
    f32 = jnp.float32
    bf16 = jnp.bfloat16
    whole = lambda e: (0, 0)
    weights = pl.BlockSpec((1, units, width), lambda e: (e, 0, 0))
    tile = pl.BlockSpec((1, ROWS, units), lambda e: (e, part, 0))
    wide = jax.ShapeDtypeStruct((experts, rows, units), bf16)
    return pl.pallas_call(
        functools.partial(expert_kernel, experts),
        out_shape=[
            jax.ShapeDtypeStruct((ROWS, width), bf16),
            wide,
            wide,
            wide,
            jax.ShapeDtypeStruct((8, width), f32),
        ],
        grid=(experts,),
        in_specs=[
            pl.BlockSpec((ROWS, width), whole),
            pl.BlockSpec((width, lanes), whole),
            pl.BlockSpec((ROWS, lanes), lambda e: (part, 0)),
            weights,
            weights,
            tile,
        ]
        + [pl.BlockSpec(memory_space=pl.ANY)] * len(filled),
        out_specs=[
            pl.BlockSpec((ROWS, width), whole),
            tile,
            tile,
            tile,
            pl.BlockSpec((8, width), whole),
        ],
        scratch_shapes=[
            pltpu.VMEM((ROWS, width), f32),
            pltpu.VMEM((ROWS, lanes), f32),
            pltpu.VMEM((ROWS, lanes), f32),
        ],
        input_output_aliases={6 + at: 1 + at for at in range(len(filled))},
        compiler_params=pltpu.CompilerParams(vmem_limit_bytes=VMEM_LIMIT),
        cost_estimate=pl.CostEstimate(
            flops=8 * experts * ROWS * units * width,
            bytes_accessed=experts * units * (4 * width + 10 * ROWS) + 4 * ROWS * width,
            transcendentals=experts * ROWS * units,
        ),
    )(h_part, router_wide, keep_wide, w_gate, w_up, back, *filled)


def weight_grads_kernel(first_ref, left_ref, low_ref, high_ref, *rest):
    out = rest[-1]
    left = left_ref[0]
    part = dot_tn(left[:ROWS], low_ref[...]) + dot_tn(left[ROWS:], high_ref[...])
    part = part[: out.shape[1]]
    if len(rest) > 1:
        part = part + rest[0][0].astype(jnp.float32)
    out[0] = part.astype(out.dtype)


def weight_grads(first, count, real, left, rights, arrived):
    _, rows, units = left.shape
    width = rights[0].shape[1]
    parts = [
        pl.BlockSpec((ROWS, width), lambda e, first, at=at: (at, 0))
        for at in ((0, 0) if rights[0].shape[0] == ROWS else (0, 1))
    ]
    out = pl.BlockSpec((1, real, width), lambda e, first: (e, 0, 0))
    return pl.pallas_call(
        weight_grads_kernel,
        out_shape=jax.ShapeDtypeStruct((count, real, width), jnp.bfloat16),
        grid_spec=pltpu.PrefetchScalarGridSpec(
            num_scalar_prefetch=1,
            grid=(count,),
            in_specs=[pl.BlockSpec((1, rows, units), lambda e, first: (first[0] + e, 0, 0))]
            + parts
            + [out] * len(arrived),
            out_specs=out,
        ),
        compiler_params=pltpu.CompilerParams(vmem_limit_bytes=VMEM_LIMIT),
        cost_estimate=pl.CostEstimate(
            flops=count * rows * units * width // 4,
            bytes_accessed=rows * width,
            transcendentals=0,
        ),
    )(first, left, *rights, *arrived)


def kept_choices(group_routes, experts, capacity):
    count, top_count = group_routes.shape
    flat = group_routes.T.reshape(-1)
    hot = (flat[:, None] == jnp.arange(experts, dtype=jnp.int32)[None, :]).astype(jnp.int32)
    earlier = jnp.cumsum(hot, axis=0) - hot
    kept = jnp.where(earlier < capacity, hot, 0)
    return jnp.sum(kept.reshape(top_count, count, experts), axis=0).astype(jnp.float32)


def on_device(
    layer_in,
    gain_one,
    w_query,
    w_key,
    w_value,
    w_out,
    bias_table,
    gain_two,
    w_router,
    w_gate,
    w_up,
    w_down,
    lengths,
    block_perm,
    buckets,
    routes,
    cotangent,
):
    tp_count = lax.axis_size("tp")
    ctx_count = lax.axis_size("ctx")
    tp_index = lax.axis_index("tp")
    ctx_index = lax.axis_index("ctx")
    rows_dev = layer_in.shape[0]
    width = layer_in.shape[1]
    group_rows = rows_dev * tp_count
    width_loc = w_query.shape[1]
    head_count = width_loc // DH
    blocks_group = group_rows // BLOCK
    experts = w_gate.shape[0]
    top_count = routes.shape[1]
    capacity = 5 * top_count * group_rows // (4 * experts)
    units = w_gate.shape[2]
    core = ctx_index % 2
    bucket_count = bias_table.shape[0]
    f32 = jnp.float32
    bf16 = jnp.bfloat16
    x_float = layer_in.astype(f32)
    inv_one = lax.rsqrt(jnp.mean(x_float * x_float, axis=1, keepdims=True) + EPS)
    normed_one = x_float * inv_one
    h_one = (normed_one * gain_one).astype(bf16)
    h_one_all = lax.all_gather(h_one, "tp", axis=0, tiled=True)
    gate_wide = pad_units(jnp.swapaxes(w_gate, 1, 2), 1)
    up_wide = pad_units(jnp.swapaxes(w_up, 1, 2), 1)
    down_wide = pad_units(w_down, 1)
    h_one_all, w_out_own, cotangent_own, gate_wide, up_wide, down_wide = (
        lax.optimization_barrier(
            (h_one_all, w_out, cotangent, gate_wide, up_wide, down_wide)
        )
    )

    def turned(x, axis, step):
        size = lax.axis_size(axis)
        return lax.ppermute(x, axis, [(at, (at + step) % size) for at in range(size)])

    def crossed(x, axis, bits):
        size = lax.axis_size(axis)
        return lax.ppermute(x, axis, [(at, at ^ bits) for at in range(size)])

    def tp_scatter(x):
        chunks = x.reshape((tp_count, x.shape[0] // tp_count) + x.shape[1:])
        pieces = [lax.dynamic_index_in_dim(chunks, tp_index, 0, False)]
        for step in range(1, tp_count):
            chunk = lax.dynamic_index_in_dim(chunks, (tp_index + step) % tp_count, 0, False)
            pieces.append(turned(chunk, "tp", step))
        return pieces

    def summed(pieces):
        total = pieces[0].astype(f32)
        for piece in pieces[1:]:
            total = total + piece.astype(f32)
        return total

    chips = ctx_count // 2
    chip = ctx_index // 2

    def core_scatter(x):
        half = x.shape[0] // 2
        away = lax.dynamic_slice_in_dim(x, (1 - core) * half, half, 0)
        mine = lax.dynamic_slice_in_dim(x, core * half, half, 0)
        return (mine.astype(f32) + crossed(away, "ctx", 1).astype(f32)).astype(bf16)

    def chip_scatter(x):
        chunks = x.reshape((chips, x.shape[0] // chips) + x.shape[1:])
        total = lax.dynamic_index_in_dim(chunks, chip, 0, False).astype(f32)
        for bits in range(1, chips):
            chunk = lax.dynamic_index_in_dim(chunks, chip ^ bits, 0, False)
            total = total + crossed(chunk, "ctx", 2 * bits).astype(f32)
        return total.astype(bf16)

    def chip_gather(x):
        result = jnp.zeros((chips,) + x.shape, x.dtype)
        result = lax.dynamic_update_index_in_dim(result, x, chip, 0)
        for bits in range(1, chips):
            got = crossed(x, "ctx", 2 * bits)
            result = lax.dynamic_update_index_in_dim(result, got, chip ^ bits, 0)
        return result.reshape((chips * x.shape[0],) + x.shape[1:])

    w_out_all = lax.all_gather(w_out_own, "tp", axis=0, tiled=True)
    half_rows = rows_dev // 2

    def by_half(x):
        split = x.reshape((tp_count, 2, half_rows) + x.shape[1:])
        return jnp.swapaxes(split, 0, 1).reshape(x.shape)

    def by_device(x):
        split = x.reshape((2, tp_count, half_rows) + x.shape[1:])
        return jnp.swapaxes(split, 0, 1).reshape(x.shape)

    grad_all = by_half(lax.all_gather(cotangent_own, "tp", axis=0, tiled=True))
    team = ctx_count // head_count
    member = ctx_index % team
    my_head = ctx_index // team
    pair_count = blocks_group // team
    slot_blocks = ctx_count * pair_count
    total = ctx_count * group_rows
    pair_ids_m = jnp.arange(pair_count, dtype=jnp.int32)
    turn = (ctx_index + pair_ids_m) % team
    ends = jnp.cumsum(lengths)
    begins = ends - lengths
    places = jnp.arange(total, dtype=jnp.int32)
    seq_start = jnp.max(
        jnp.where(begins[None, :] <= places[:, None], begins[None, :], 0), axis=1
    ).reshape(total // BLOCK, BLOCK)
    low_block = seq_start[:, 0] // BLOCK
    high_start = seq_start[:, BLOCK - 1]
    thresholds = jnp.sum(
        (buckets[None, :] < jnp.arange(bucket_count, dtype=jnp.int32)[:, None]).astype(jnp.int32),
        axis=1,
    )
    head_hot = (jnp.arange(head_count, dtype=jnp.int32) == my_head).astype(f32)
    my_table = jnp.sum(bias_table * head_hot[None, :], axis=1)
    near_table = (my_table - my_table[bucket_count - 1]) * LOG2E
    sources = jnp.arange(ctx_count, dtype=jnp.int32)
    members = (member + jnp.arange(team, dtype=jnp.int32)) % team
    half_of = (members[:, None, None] + sources[None, :, None] + pair_ids_m[None, None, :]) % team
    perm_pairs = block_perm.reshape(1, ctx_count, pair_count, team)
    natural = jnp.sum(
        jnp.where(
            half_of[..., None] == jnp.arange(team, dtype=jnp.int32)[None, None, None, :],
            perm_pairs,
            0,
        ),
        axis=3,
    ).reshape(-1)
    own_natural = natural[:slot_blocks]
    rank = jnp.sum((own_natural[None, :] < own_natural[:, None]).astype(jnp.int32), axis=1)
    slots = jnp.arange(slot_blocks, dtype=jnp.int32)
    order = jnp.sum(jnp.where(rank[None, :] == slots[:, None], slots[None, :], 0), axis=1)
    scalars = (natural, order, low_block, high_start, thresholds, near_table)

    def to_heads(x, kinds):
        split = x.reshape(kinds, head_count, DH, pair_count, team, BLOCK)
        split = turn_halves(split, 3, turn, 1)
        send = split.transpose(1, 4, 3, 0, 2, 5).reshape(
            ctx_count, pair_count, kinds * DH, BLOCK
        )
        got = lax.all_to_all(send, "ctx", 0, 0, tiled=True)
        return got.reshape(slot_blocks, kinds * DH, BLOCK)

    def from_heads(x, kinds):
        send = x.reshape(ctx_count, pair_count, kinds * DH, BLOCK)
        got = lax.all_to_all(send, "ctx", 0, 0, tiled=True)
        split = got.reshape(head_count, team, pair_count, kinds, DH, BLOCK)
        split = split.transpose(3, 0, 4, 2, 1, 5)
        split = turn_halves(split, 3, turn, -1)
        return split.reshape(kinds * head_count * DH, group_rows)

    def team_shift(x, step):
        route = []
        for device in range(ctx_count):
            base = device // team * team
            route.append((device, base + (device % team + step) % team))
        return lax.ppermute(x, "ctx", route)

    direct = pair_count == tp_count
    spot = (ctx_index + tp_index) % team

    def rows_from_heads(x):
        if direct:
            got = lax.all_to_all(x, ("ctx", "tp"), 0, 0, tiled=True)
            split = got.reshape(head_count, 1, team, tp_count, DH, BLOCK)
            split = turn_halves(split, 1, spot[None], -1)
            split = split.transpose(3, 0, 4, 1, 2, 5)
        else:
            split = from_heads(x, 1).reshape(width_loc, tp_count, rows_dev)
            split = lax.all_to_all(split.transpose(1, 0, 2), "tp", 0, 0, tiled=True)
        return split.reshape(tp_count * width_loc, rows_dev)

    def heads_from_rows(x):
        if direct:
            split = x.reshape(tp_count, head_count, DH, 1, team, BLOCK)
            split = split.transpose(1, 3, 4, 0, 2, 5)
            split = turn_halves(split, 1, spot[None], 1)
            send = split.reshape(ctx_count * tp_count, DH, BLOCK)
            return lax.all_to_all(send, ("ctx", "tp"), 0, 0, tiled=True)
        send = x.reshape(tp_count, width_loc, rows_dev)
        got = lax.all_to_all(send, "tp", 0, 0, tiled=True)
        return to_heads(got.transpose(1, 0, 2).reshape(width_loc, group_rows), 1)

    w_heads = (w_query, w_key, w_value)
    send = project(turn, h_one_all, w_heads, head_count, team)
    own_qkv = lax.all_to_all(
        send.reshape(ctx_count, pair_count, 3 * DH, BLOCK), "ctx", 0, 0, tiled=True
    ).reshape(slot_blocks, 3 * DH, BLOCK)
    own_pairs = own_qkv[:, DH:, :]
    parts = [own_qkv] + [team_shift(own_pairs, -step) for step in range(1, team)]
    head_block = (slot_blocks, DH, BLOCK)
    att_slots, att_full, log_total = attention_call(
        forward_kernel,
        team,
        bucket_count,
        scalars,
        seq_start,
        parts,
        [
            jax.ShapeDtypeStruct(head_block, bf16),
            jax.ShapeDtypeStruct(head_block, f32),
            jax.ShapeDtypeStruct((slot_blocks, BLOCK), f32),
        ],
        total,
        [],
        8,
    )
    attended_rows = rows_from_heads(att_slots)
    mixed_in = x_float + lax.dot_general(
        attended_rows, w_out_all, (((0,), (0,)), ((), ())), preferred_element_type=f32
    )
    inv_two = lax.rsqrt(jnp.mean(mixed_in * mixed_in, axis=1, keepdims=True) + EPS)
    normed_two = mixed_in * inv_two
    h_two = (normed_two * gain_two).astype(bf16)
    h_two_parts = [
        lax.all_gather(h_two[at : at + half_rows], "tp", axis=0, tiled=True)
        for at in (0, half_rows)
    ]
    lanes = BLOCK
    keep = by_half(kept_choices(routes, experts, capacity))
    keep_wide = jnp.pad(keep, ((0, 0), (0, lanes - experts)))
    router_wide = jnp.pad(w_router, ((0, 0), (0, lanes - experts)))
    back = jnp.einsum("rd,efd->erf", grad_all, down_wide, preferred_element_type=f32)
    filled, d_h_two, router_parts = [], [], []
    for part, h_part in enumerate(h_two_parts):
        d_h_part, *filled, router_part = expert_layer(
            part, h_part, router_wide, keep_wide, gate_wide, up_wide, back, filled
        )
        router_parts.append(router_part)
        d_h_two.append(
            lax.psum_scatter(d_h_part, "tp", scatter_dimension=0, tiled=True)
        )
    hidden, d_gate_bf, d_up_bf = filled
    hidden, d_up_bf, d_h_two[0] = lax.optimization_barrier((hidden, d_up_bf, d_h_two[0]))
    some = experts // 2
    core_first = (core * some).astype(jnp.int32).reshape(1)
    away_first = ((1 - core) * some).astype(jnp.int32).reshape(1)
    operands = (
        (d_gate_bf, h_two_parts),
        (d_up_bf, h_two_parts),
        (hidden, (grad_all, grad_all)),
    )
    away = [
        weight_grads(away_first, some, units, left, rights, ()) for left, rights in operands
    ]
    mine = [
        weight_grads(core_first, some, units, left, rights, (crossed(grads, "ctx", 1),))
        for (left, rights), grads in zip(operands, away)
    ]
    d_h_two, _ = lax.optimization_barrier((d_h_two, mine))
    d_h_two = jnp.concatenate(d_h_two, axis=0).astype(f32)
    same_core = [list(range(first, ctx_count, 2)) for first in range(2)]
    def both_halves(grads):
        other = crossed(grads, "ctx", 1)
        first = jnp.where(core == 0, grads, other)
        second = jnp.where(core == 0, other, grads)
        return jnp.concatenate([first, second], axis=0).astype(f32)

    mine = lax.psum(tuple(mine), "ctx", axis_index_groups=same_core)
    grad_float = cotangent.astype(f32)
    grad_router_part = (router_parts[0] + router_parts[1])[:experts]
    d_norm_two = d_h_two * gain_two
    grad_gain_two_part = jnp.sum(d_h_two * normed_two, axis=0)
    d_mixed = grad_float + inv_two * (
        d_norm_two - normed_two * jnp.mean(d_norm_two * normed_two, axis=1, keepdims=True)
    )
    d_attn = d_mixed.astype(bf16)
    d_attended = lax.dot_general(
        w_out_all, d_attn, (((1,), (1,)), ((), ())), preferred_element_type=f32
    ).astype(bf16)
    d_att_slots = heads_from_rows(d_attended)
    hidden, d_attn = lax.optimization_barrier((hidden, d_attn))
    mixed_part = jnp.einsum(
        "ecf,efd->cd", hidden[:, :, :units], w_down, preferred_element_type=f32
    )
    out_part = jnp.dot(attended_rows, d_attn, preferred_element_type=f32)
    d_att_slots, mixed_part, out_part = lax.optimization_barrier(
        (d_att_slots, by_device(mixed_part.astype(bf16)), out_part.astype(bf16))
    )
    out_pieces = tp_scatter(out_part)
    pair_block = jax.ShapeDtypeStruct((slot_blocks, 2 * DH, BLOCK), bf16)
    back_out = attention_call(
        backward_kernel,
        team,
        bucket_count,
        scalars,
        seq_start,
        parts + [d_att_slots, att_full, log_total],
        [jax.ShapeDtypeStruct(head_block, bf16)]
        + [pair_block] * team
        + [jax.ShapeDtypeStruct((1, BLOCK), f32)],
        total,
        [
            pltpu.VMEM((total + BLOCK, 2 * DH), f32),
            pltpu.VMEM((2 * BLOCK, BLOCK), f32),
        ],
        BACK_COST,
    )
    out_pieces, back_out = lax.optimization_barrier((out_pieces, tuple(back_out)))
    pair_grads = back_out[1].astype(f32)
    for step in range(1, team):
        pair_grads = pair_grads + team_shift(back_out[1 + step], step).astype(f32)
    send = jnp.concatenate([back_out[0], pair_grads.astype(bf16)], axis=1)
    got = lax.all_to_all(
        send.reshape(ctx_count, pair_count, 3 * DH, BLOCK), "ctx", 0, 0, tiled=True
    )
    grad_out = summed(out_pieces)
    small_rows = 16 * chips
    table_part = back_out[1 + team][0, :bucket_count, None] * head_hot[None, :]
    table_row = jnp.pad(table_part.reshape(1, -1), ((0, 0), (0, width - table_part.size)))
    small = jnp.concatenate(
        [
            jnp.zeros((1, width), f32),
            grad_gain_two_part[None],
            grad_router_part,
            table_row,
            jnp.zeros((small_rows - 3 - experts, width), f32),
        ],
        axis=0,
    )
    d_h_one_part, wide = unproject(
        turn,
        got.reshape(head_count, team, pair_count, 3 * DH, BLOCK),
        h_one_all,
        w_heads,
        grad_out.astype(bf16),
        small,
        gain_one[None],
    )
    d_h_pieces = tp_scatter(d_h_one_part)
    wide = chip_scatter(core_scatter(wide))
    wide, d_h_pieces = lax.optimization_barrier((wide, d_h_pieces))
    mine, mixed_part, _ = lax.optimization_barrier((mine, mixed_part, wide))
    mixed_rows = lax.psum_scatter(mixed_part, "tp", scatter_dimension=0, tiled=True)
    layer_out = mixed_in + mixed_rows.astype(f32)
    others = [crossed(grads, "ctx", 1) for grads in mine]
    expert_grads = place_half(core_first, mine, [])
    wide, expert_grads = lax.optimization_barrier((chip_gather(wide), expert_grads))
    expert_grads = place_half(away_first, others, expert_grads)
    d_h_one = summed(d_h_pieces)
    d_norm_one = d_h_one * gain_one
    grad_x = d_mixed + inv_one * (
        d_norm_one - normed_one * jnp.mean(d_norm_one * normed_one, axis=1, keepdims=True)
    )
    wide = both_halves(wide)
    grad_qkv = wide[: 3 * width_loc].T
    grad_out = wide[3 * width_loc : 4 * width_loc]
    small = wide[4 * width_loc :]
    over_rows = small[: 2 + experts]
    own = width // tp_count
    slices = over_rows.reshape(2 + experts, tp_count, own).transpose(1, 0, 2)
    over_rows = summed(tp_scatter(slices.reshape(-1, own)))
    gain_one_grad = over_rows[0]
    gain_two_grad = over_rows[1]
    router_grad = over_rows[2:].T
    table_grad = small[2 + experts, : bucket_count * head_count].reshape(
        bucket_count, head_count
    )
    return (
        layer_out,
        grad_x,
        gain_one_grad,
        grad_qkv[:, :width_loc],
        grad_qkv[:, width_loc : 2 * width_loc],
        grad_qkv[:, 2 * width_loc :],
        grad_out,
        table_grad,
        gain_two_grad,
        router_grad,
        jnp.swapaxes(expert_grads[0], 1, 2),
        jnp.swapaxes(expert_grads[1], 1, 2),
        expert_grads[2],
    )


def solution(mesh):
    placed = (
        P(("ctx", "tp"), None),
        P(),
        P(None, "tp"),
        P(None, "tp"),
        P(None, "tp"),
        P("tp", None),
        P(None, "tp"),
        P(),
        P(),
        P(None, None, "tp"),
        P(None, None, "tp"),
        P(None, "tp", None),
        P(),
        P(),
        P(),
        P("ctx", None),
        P(("ctx", "tp"), None),
    )
    return jax.shard_map(
        on_device,
        mesh=mesh,
        in_specs=placed,
        out_specs=(
            P(("ctx", "tp"), None),
            P(("ctx", "tp"), None),
            P("tp"),
            P(None, "tp"),
            P(None, "tp"),
            P(None, "tp"),
            P("tp", None),
            P(None, "tp"),
            P("tp"),
            P("tp", None),
            P(None, None, "tp"),
            P(None, None, "tp"),
            P(None, "tp", None),
        ),
        check_vma=False,
    )
```
